256 devices in a mesh: row: 8 (over z_lo, y), col: 32 (over z_hi, x, core).
Axes of the slice: x: 4, y: 4, z: 8 (z_hi: 4, z_lo: 2; z = z_hi * 2 + z_lo), core: 2. Of those that a mesh axis runs over, the one named last changes fastest.
Arguments:
- stream: bfloat16 [1024, 8192], P('row', 'col'), may hold values from -36 to 36
- heads_out: bfloat16 [1024, 8192], P('row', 'col'), may hold values from -6 to 6
- w_out: bfloat16 [8192, 8192], P('row', 'col'), may hold values from -0.0625 to 0.0625
- norm_gain: float32 [8192], replicated, may hold values from 0.1 to 1.9
- expert_ids: int32 [1024, 2], P('row'), may hold values from 0 to 15, all different within a row; in each aligned block of 128 rows (0 to 127, 128 to 255, ...) at most 32 rows name the same one
- route_gates: float32 [1024, 2], P('row'), may hold values from 0.2 to 1
- w_gate: bfloat16 [8192, 65536], P(None, ('row', 'col')), may hold values from -0.0625 to 0.0625
- w_up: bfloat16 [8192, 65536], P(None, ('row', 'col')), may hold values from -0.0625 to 0.0625
- w_down: bfloat16 [65536, 8192], P(('row', 'col')), may hold values from -0.09375 to 0.09375
Outputs:
- mixed: bfloat16 [1024, 8192], P('row', 'col')
The draws below stay inside these ranges and needn't reach their ends.
Inputs may be any that keep to these rules, and one draw needn't show every extreme that they name: `expert_ids`: each row names two different experts. Within the 128 rows of one index of row no expert is named more than 32 times, and in some such block an expert is named exactly 32 times.
All inputs are finite; a program needn't handle non-finite values.
Results may differ from the reference program's by a relative error of at most 0.011.
Values may be sent and summed in bfloat16 or wider, within the bound.
A program may use at most 128 MiB of HBM per device.

```python
import math
import jax
import jax.numpy as jnp
import numpy as np
from jax import lax

D = 8192
H = 4096
TOK_ROW = 128
EXPERTS = 16
TOKENS = 1024
CAP = 32
H_DEV = 256


def draw_stream(key, part):
    key = jax.random.fold_in(key, 11)
    key_base, key_rows, key_cols = jax.random.split(key, 3)
    base_values = jnp.clip(jax.random.normal(key_base, (TOKENS, D), jnp.float32), -4.0, 4.0)
    low_end = 0.3
    high_end = 3.0
    row_scale = jnp.exp(jax.random.uniform(key_rows, (TOKENS, 1), jnp.float32, math.log(low_end), math.log(high_end)))
    col_scale = jnp.exp(jax.random.uniform(key_cols, (1, D), jnp.float32, math.log(low_end), math.log(high_end)))
    return (base_values * row_scale * col_scale).astype(jnp.bfloat16)


def block_levels(rng, extent, cuts, smallest, largest):
    level, own = 1.0, jax.random.fold_in(rng, 6)
    for dim, blocks in cuts:
        heights = jnp.exp(jax.random.uniform(jax.random.fold_in(own, dim), (blocks,), jnp.float32, smallest / len(cuts), largest / len(cuts)))
        level = level * jnp.repeat(heights, extent[dim] // blocks).reshape([-1 if axis == dim else 1 for axis in range(len(extent))])
    return level


def deal_out(stream_key, own, number, rows, count, top, bound, lean):
    ranking = jax.random.permutation(stream_key, count)
    packed, common = shares(count, rows * top, bound, lean, True), shares(count, rows * top, bound, lean, False)
    places = jnp.arange(count)

    def named(tallies, offset_by):
        used = int((tallies > 0).sum())
        fixed = max(1, used // 4)
        passed = fixed + (places - fixed + offset_by * (used - fixed)) % max(1, count - fixed)
        return jnp.zeros((count,), jnp.int32).at[ranking[jnp.where(places < fixed, places, passed)]].set(jnp.asarray(tallies, jnp.int32))

    tallies = jnp.where(number % 4 == 0, named(packed, number // 4), named(common, number - number // 4 - 1))
    mixed = jax.random.permutation(jax.random.fold_in(own, 3), count)
    source_of, sink = mixed[0:count // 2 * 2:2], mixed[1:count // 2 * 2:2]
    room = jnp.minimum(tallies[source_of] - 1, bound - tallies[sink]) // 2
    room = jnp.where((source_of == ranking[0]) | (sink == ranking[0]) | (tallies[sink] == 0), 0, jnp.maximum(room, 0))
    passed = jax.random.randint(jax.random.fold_in(own, 4), (count // 2,), 0, 1 << 20) % (room + 1)
    tallies = tallies.at[source_of].add(-passed).at[sink].add(passed)
    members = jnp.searchsorted(jnp.cumsum(tallies), jnp.arange(rows * top), side="right").astype(jnp.int32)
    table = members.reshape(top, rows).T
    table = table[jax.random.permutation(jax.random.fold_in(own, 1), rows)]
    offset_by = jax.random.randint(jax.random.fold_in(own, 2), (rows, 1), 0, top)
    return jnp.take_along_axis(table, (jnp.arange(top)[None, :] + offset_by) % top, axis=1)


def shares(number_of, total, reach, lean, full):
    loads = [(1 << 20) // math.isqrt(standing ** lean) + 1 for standing in range(1, number_of + 1)]
    largest = reach if full else min(reach, max(-(-total // number_of), total * loads[0] // sum(loads)))
    least = 1 if total - largest >= number_of - 1 else 0
    holding, surplus = [largest] + [least] * (number_of - 1), total - largest - least * (number_of - 1)
    while surplus > 0:
        free = [i for i in range(1, number_of) if holding[i] < largest] or [i for i in range(1, number_of) if holding[i] < reach]
        pool, remaining = sum([loads[i] for i in free]), surplus
        for i in free:
            more = min(reach - holding[i], max(1, remaining * loads[i] // pool), surplus)
            holding[i] = holding[i] + more
            surplus = surplus - more
    return np.array(holding)


def bell_draw(rng, extent, deviation, limit, shards=(), held_as=jnp.bfloat16):
    result = jax.random.normal(rng, extent, jnp.float32) * deviation
    if len(shards) > 0:
        result = block_levels(rng, extent, shards, -0.22, 0.18) * result
    return jnp.clip(result, min=-limit, max=limit).astype(held_as)


def setup_inputs(seed: int = 0) -> dict:
    seeds = jax.random.split(jax.random.key(seed), 10)
    stream = draw_stream(jax.random.fold_in(seeds[9], 71), 0)
    heads_out = bell_draw(seeds[1], (TOKENS, D), 1.0, 6.0, ((0, 8), (1, 32)))
    w_out = bell_draw(seeds[2], (D, D), D ** -0.5, 0.0625, ((0, 8), (1, 32)))
    norm_gain = jnp.clip(1.0 + 0.18 * jax.random.normal(seeds[3], (D,), jnp.float32), 0.1, 1.9)
    expert_ids_keys = jax.random.split(jax.random.fold_in(seeds[4], 1), TOKENS // TOK_ROW)
    expert_ids_turns = jax.random.permutation(jax.random.fold_in(seeds[4], 3), TOKENS // TOK_ROW)
    expert_ids = jax.vmap(lambda own, number: deal_out(jax.random.fold_in(seeds[4], 2), own, number, TOK_ROW, EXPERTS, 2, CAP, 2))(expert_ids_keys, expert_ids_turns).reshape((TOKENS, 2))
    route_gates = jnp.clip(0.2 + 0.8 * jax.random.uniform(seeds[5], (TOKENS, 2), jnp.float32) ** block_levels(seeds[5], (TOKENS, 2), ((0, 8),), -0.2, 0.2), 0.2, 1.0)
    w_gate = bell_draw(seeds[6], (D, EXPERTS * H), D ** -0.5, 0.0625, ((1, 256),))
    w_up = bell_draw(seeds[7], (D, EXPERTS * H), D ** -0.5, 0.0625, ((1, 256),))
    w_down = bell_draw(seeds[8], (EXPERTS * H, D), H ** -0.5, 0.09375, ((0, 256),))
    return dict(stream=stream, heads_out=heads_out, w_out=w_out, norm_gain=norm_gain, expert_ids=expert_ids, route_gates=route_gates, w_gate=w_gate, w_up=w_up, w_down=w_down)


def normalize(values, gain):
    wide = values.astype(jnp.float32)
    square = lax.optimization_barrier(jnp.mean(wide * wide, axis=-1, keepdims=True))
    return (wide * lax.rsqrt(square + 1e-05) * gain).astype(jnp.bfloat16)

def slot_positions(expert_ids, block_rows, expert_count):
    one_hot = (expert_ids[:, :, None] == jnp.arange(expert_count, dtype=jnp.int32)).astype(jnp.int32)
    grouped = one_hot.reshape(-1, block_rows * 2, expert_count)
    earlier = jnp.cumsum(grouped, axis=1) - grouped
    return lax.optimization_barrier(jnp.sum(earlier * grouped, axis=-1)).reshape(expert_ids.shape).astype(jnp.int32)

def reference(stream, heads_out, w_out, norm_gain, expert_ids, route_gates, w_gate, w_up, w_down):
    projected = jnp.dot(heads_out, w_out, preferred_element_type=jnp.float32)
    residual = (stream.astype(jnp.float32) + projected).astype(jnp.bfloat16)
    normed = normalize(residual, norm_gain)
    token_count = residual.shape[0]
    blocks = token_count // TOK_ROW
    position = slot_positions(expert_ids, TOK_ROW, EXPERTS)
    both_ones = jnp.ones((1, 2), jnp.int32)
    token_ids = jnp.arange(token_count, dtype=jnp.int32)[:, None] * both_ones
    block_of = (jnp.arange(token_count, dtype=jnp.int32) // TOK_ROW)[:, None] * both_ones
    table = jnp.zeros((EXPERTS, blocks, CAP), jnp.int32).at[expert_ids, block_of, position].set(token_ids)
    filled = jnp.zeros((EXPERTS, blocks, CAP), jnp.bfloat16).at[expert_ids, block_of, position].set(1.0)
    slot_rows = jnp.take(normed, table.reshape(EXPERTS * blocks * CAP), axis=0).reshape(EXPERTS, blocks * CAP, D)
    slot_rows = slot_rows * filled.reshape(EXPERTS, blocks * CAP, 1)
    block_count = H // H_DEV

    def run_expert(index):
        rows_in = lax.dynamic_index_in_dim(slot_rows, index, 0, keepdims=False)
        gate_mat = lax.dynamic_slice_in_dim(w_gate, index * H, H, 1)
        up_mat = lax.dynamic_slice_in_dim(w_up, index * H, H, 1)
        down_mat = lax.dynamic_slice_in_dim(w_down, index * H, H, 0)
        gate_pre = jnp.dot(rows_in, gate_mat, preferred_element_type=jnp.float32)
        up_pre = jnp.dot(rows_in, up_mat, preferred_element_type=jnp.float32)
        activated = (jax.nn.silu(gate_pre) * up_pre).astype(jnp.bfloat16)
        pieces = activated.reshape(rows_in.shape[0], block_count, H_DEV).transpose(1, 0, 2)
        downs = down_mat.reshape(block_count, H_DEV, D)

        def add_block(accum_sum, pair):
            partial_value = jnp.dot(pair[0], pair[1], preferred_element_type=jnp.float32)
            rounded = lax.optimization_barrier(partial_value.astype(jnp.bfloat16))
            return (accum_sum + rounded.astype(jnp.float32), None)
        summed, leftover = lax.scan(add_block, jnp.zeros((rows_in.shape[0], D), jnp.float32), (pieces, downs))
        return summed.astype(jnp.bfloat16)
    expert_out = lax.map(run_expert, jnp.arange(EXPERTS, dtype=jnp.int32))
    picked = expert_out[expert_ids, block_of * CAP + position].astype(jnp.float32)
    mixed = residual.astype(jnp.float32) + lax.optimization_barrier(jnp.sum(route_gates[:, :, None] * picked, axis=1))
    return mixed.astype(jnp.bfloat16)
```

```python
import jax
import jax.numpy as jnp
from jax import lax
from jax.experimental import pallas as pl
from jax.experimental.pallas import tpu as pltpu
from jax.sharding import PartitionSpec as P

MESH = pl.DeviceIdType.MESH
BF = jnp.bfloat16
F32 = jnp.float32
WIDTH = 8192
CHUNK_ORDER_IN = (0, 1, 3, 2)
CHUNK_ORDER_OUT = (2, 1, 3, 0)


def place(z_lo, y, z_hi, x, core):
    return (z_lo * 4 + y, z_hi * 8 + x * 2 + core)


def local_copy(src, dst, sem):
    copy = pltpu.make_async_copy(src, dst, sem)
    copy.start()


def send(src, dst, send_sem, recv_sem, device):
    copy = pltpu.make_async_remote_copy(
        src_ref=src,
        dst_ref=dst,
        send_sem=send_sem,
        recv_sem=recv_sem,
        device_id=device,
        device_id_type=MESH,
    )
    copy.start()


def wait_bytes(view, sem):
    pltpu.make_async_copy(view, view, sem).wait()


def dot(a, b):
    return jnp.dot(a, b, preferred_element_type=F32)


def kernel(
    stream, heads, w_out, gain, ids, gates, w_gate, w_up, w_down,
    out,
    heads_in, w_out_pair, proj_out, proj_in, stream_v, gate_w, up_w, down_w,
    payload, tokens, pre, pre_in, squares, squares_in, act,
    far_out, right_out, left_out, far_left, far_right, from_left, from_right, summed, final_in,
    in_sem, w_sem, wr_sem, ws_sem,
    p1_recv, p1_send, px_recv, px_send, rs_recv, rs_send,
    d1_recv, d1_send, d2_recv, d2_send, d3_recv, d3_send, ex_recv, ex_send,
    f_recv, f_send, g_recv, g_send, z_recv, z_send,
):
    row = lax.axis_index("row")
    col = lax.axis_index("col")
    z_lo, y = lax.div(row, 4), lax.rem(row, 4)
    z_hi = lax.div(col, 8)
    x = lax.rem(lax.div(col, 2), 4)
    core = lax.rem(col, 2)
    other = 1 - core
    right = lax.rem(x + 1, 4)
    left = lax.rem(x + 3, 4)
    far = lax.rem(x + 2, 4)
    right_dev = place(z_lo, y, z_hi, right, core)
    left_dev = place(z_lo, y, z_hi, left, core)
    pair_dev = place(z_lo, y, z_hi, x, other)

    own_group = lax.rem(x, 2) * 2 + core
    p_row_lo = lax.div(z_hi, 2)
    p_row_y = lax.rem(z_hi, 2) * 2 + lax.div(x, 2)
    p_self = jnp.logical_and(jnp.logical_and(p_row_lo == z_lo, p_row_y == y), z_lo == core)
    for dz in (2, 1, 3, 0):
        for dx in (2, 1, 3, 0):
            to_x = lax.rem(x + dx, 4)
            to_z = lax.rem(z_hi + dz, 4)
            src = heads.at[pl.ds(to_x * 32, 32), :]
            dst = heads_in.at[to_x, own_group, y]
            device = place(p_row_lo, p_row_y, to_z, to_x, z_lo)
            if dz == 0 and dx == 0:
                @pl.when(p_self)
                def _():
                    local_copy(src, dst, p1_recv)

                @pl.when(jnp.logical_not(p_self))
                def _():
                    send(src, dst, p1_send.at[1], p1_recv, device)
            else:
                send(src, dst, p1_send.at[0], p1_recv, device)

    local_copy(w_out, w_out_pair.at[core], w_sem.at[0])
    send(w_out, w_out_pair.at[core], ws_sem.at[0], wr_sem.at[0], pair_dev)
    local_copy(stream, stream_v, in_sem.at[0])
    local_copy(w_gate.at[:, core], gate_w.at[core], w_sem.at[1])
    local_copy(w_up.at[:, core], up_w.at[core], w_sem.at[2])
    send(w_gate.at[:, other], gate_w.at[core], ws_sem.at[1], wr_sem.at[1], pair_dev)
    send(w_up.at[:, other], up_w.at[core], ws_sem.at[2], wr_sem.at[2], pair_dev)

    def load_down(b, carry):
        mine = pl.multiple_of((2 * b + core) * 256, 256)
        theirs = pl.multiple_of((2 * b + other) * 256, 256)
        local_copy(w_down.at[:, pl.ds(mine, 256)], down_w.at[core, b], w_sem.at[3])
        send(w_down.at[:, pl.ds(theirs, 256)], down_w.at[core, b], ws_sem.at[3], wr_sem.at[3], pair_dev)
        return carry

    lax.fori_loop(0, 16, load_down, 0)

    lane = lax.broadcasted_iota(jnp.int32, (128, 128), 1)
    sub = lax.broadcasted_iota(jnp.int32, (128, 128), 0)
    first = (ids[:, 0:1] == lane).astype(F32)
    second = (ids[:, 1:2] == lane).astype(F32)
    earlier = dot((lane < sub).astype(BF), (first + second).astype(BF))
    slot_lane = lax.broadcasted_iota(jnp.int32, (128, 512), 1)
    slot0 = ids[:, 0:1] * 32 + jnp.sum(earlier * first, axis=1, keepdims=True).astype(jnp.int32)
    slot1 = ids[:, 1:2] * 32 + jnp.sum(earlier * second, axis=1, keepdims=True).astype(jnp.int32)
    pick0 = (slot0 == slot_lane).astype(F32)
    pick1 = (slot1 == slot_lane).astype(F32)
    spread = (pick0 + pick1).T.astype(BF)
    pre[...] = jnp.zeros_like(pre)
    squares[...] = jnp.zeros_like(squares)

    def project(group):
        rows = [heads_in[group, j].reshape(128, 256) for j in range(4)]
        for dc in range(2):
            c = core if dc == 0 else other
            total = dot(rows[0], w_out_pair[c, 0:256, :])
            for j in range(1, 4):
                total = total + dot(rows[j], w_out_pair[c, j * 256:(j + 1) * 256, :])
            proj_out[group, c] = total.astype(BF).reshape(4, 32, 256)
        for dy in (2, 1, 3, 0):
            to_y = lax.rem(y + dy, 4)
            for dc in range(2):
                c = core if dc == 0 else other
                src = proj_out.at[group, c, to_y]
                dst = proj_in.at[row, pl.ds(group * 32, 32), :]
                device = place(core, to_y, z_hi, x, c)
                if dy == 0 and dc == 0:
                    @pl.when(z_lo == core)
                    def _():
                        local_copy(src, dst, rs_recv)

                    @pl.when(z_lo != core)
                    def _():
                        send(src, dst, rs_send.at[1], rs_recv, device)
                else:
                    send(src, dst, rs_send.at[0], rs_recv, device)

    wait_bytes(heads_in.at[x], p1_recv)
    send(heads_in.at[x], heads_in.at[x], px_send.at[0], px_recv.at[0], right_dev)
    send(heads_in.at[x], heads_in.at[x], px_send.at[1], px_recv.at[1], left_dev)
    wait_bytes(w_out_pair.at[core], w_sem.at[0])
    wait_bytes(w_out_pair.at[other], wr_sem.at[0])
    project(x)
    wait_bytes(heads_in.at[left], px_recv.at[0])
    send(heads_in.at[left, 0:2], heads_in.at[left, 0:2], px_send.at[2], px_recv.at[2], right_dev)
    wait_bytes(heads_in.at[right], px_recv.at[1])
    send(heads_in.at[right, 2:4], heads_in.at[right, 2:4], px_send.at[3], px_recv.at[3], left_dev)
    project(left)
    project(right)
    wait_bytes(heads_in.at[far, 0:2], px_recv.at[2])
    wait_bytes(heads_in.at[far, 2:4], px_recv.at[3])
    project(far)

    wait_bytes(stream_v, in_sem.at[0])
    wait_bytes(proj_in, rs_recv)
    residual = stream_v[...].astype(F32)
    for r in range(8):
        residual = residual + proj_in[r].astype(F32)
    stream_v[...] = residual.astype(BF)

    payload[...] = dot(spread, stream_v[...]).astype(BF).reshape(16, 32, 256)
    for dz in CHUNK_ORDER_IN:
        to_z = lax.rem(z_hi + dz, 4)
        for dl in (1, 0):
            to_lo = z_lo if dl == 0 else 1 - z_lo
            for dy in (2, 1, 3, 0):
                to_y = lax.rem(y + dy, 4)
                expert = 2 * (to_lo * 4 + to_y) + lax.div(to_z, 2)
                src = payload.at[expert]
                dst = tokens.at[x, z_hi, row]
                if dz == 0 and dl == 0 and dy == 0:
                    local_copy(src, dst, d1_recv.at[dz])
                else:
                    send(src, dst, d1_send.at[dz], d1_recv.at[dz], place(to_lo, to_y, to_z, x, core))

    wait_bytes(gate_w.at[core], w_sem.at[1])
    wait_bytes(up_w.at[core], w_sem.at[2])
    wait_bytes(gate_w.at[other], wr_sem.at[1])
    wait_bytes(up_w.at[other], wr_sem.at[2])

    def absorb(from_x, from_z):
        block = tokens[from_x, from_z].reshape(256, 256).astype(F32)
        square = block * block
        squares[...] += square[:, 0:128] + square[:, 128:256]
        scaled = (block * gain[from_z * 8 + from_x * 2 + core]).astype(BF)
        b = from_z * 4 + from_x
        for c in range(2):
            pre[c] += dot(scaled, gate_w[c, b])
            pre[2 + c] += dot(scaled, up_w[c, b])

    def chunk_z(i):
        return lax.rem(z_hi + 4 - CHUNK_ORDER_IN[i], 4)

    def gather_first(i):
        zc = chunk_z(i)
        wait_bytes(tokens.at[x, zc], d1_recv.at[CHUNK_ORDER_IN[i]])
        view = tokens.at[x, zc]
        send(view, view, d2_send.at[0, i], d2_recv.at[0, i], right_dev)
        send(view, view, d2_send.at[1, i], d2_recv.at[1, i], left_dev)
        absorb(x, zc)

    def gather_second(i):
        zc = chunk_z(i)
        wait_bytes(tokens.at[left, zc], d2_recv.at[0, i])
        view = tokens.at[left, zc, 0:4]
        send(view, view, d3_send.at[0, i], d3_recv.at[0, i], right_dev)
        wait_bytes(tokens.at[right, zc], d2_recv.at[1, i])
        view = tokens.at[right, zc, 4:8]
        send(view, view, d3_send.at[1, i], d3_recv.at[1, i], left_dev)
        absorb(left, zc)
        absorb(right, zc)

    def gather_third(i):
        zc = chunk_z(i)
        wait_bytes(tokens.at[far, zc, 0:4], d3_recv.at[0, i])
        wait_bytes(tokens.at[far, zc, 4:8], d3_recv.at[1, i])
        absorb(far, zc)

    for i in range(6):
        if i < 4:
            gather_first(i)
        if 1 <= i < 5:
            gather_second(i - 1)
        if i >= 2:
            gather_third(i - 2)

    send(pre, pre_in, ex_send.at[0], ex_recv.at[0], pair_dev)
    send(squares, squares_in, ex_send.at[1], ex_recv.at[1], pair_dev)
    wait_bytes(squares_in, ex_recv.at[1])
    wait_bytes(pre_in, ex_recv.at[0])
    mean = jnp.sum(squares[...] + squares_in[...], axis=1, keepdims=True) / WIDTH
    scale = lax.rsqrt(mean + 1e-05)
    for c in range(2):
        gate_pre = (pre[c] + pre_in[c]) * scale
        up_pre = (pre[2 + c] + pre_in[2 + c]) * scale
        act[c] = (gate_pre / (1.0 + jnp.exp(-gate_pre)) * up_pre).astype(BF)

    wait_bytes(down_w.at[core], w_sem.at[3])
    wait_bytes(down_w.at[other], wr_sem.at[3])

    def down(start, rows, to_x, zc):
        b = zc * 4 + to_x
        return dot(act[0, start:start + rows, :], down_w[0, b]) + dot(
            act[1, start:start + rows, :], down_w[1, b]
        )

    def out_z(i):
        return lax.rem(z_hi + CHUNK_ORDER_OUT[i], 4)

    def return_first(i):
        zc = out_z(i)
        far_out[i] = down(0, 256, far, zc).astype(BF)
        send(far_out.at[i, 0:128], far_left.at[i], f_send.at[0, i], f_recv.at[0, i], right_dev)
        send(far_out.at[i, 128:256], far_right.at[i], f_send.at[1, i], f_recv.at[1, i], left_dev)
        right_out[i, 128:256] = down(128, 128, right, zc).astype(BF)
        send(right_out.at[i, 128:256], from_left.at[i, 128:256], g_send.at[0, i], g_recv.at[0, i], right_dev)
        left_out[i, 0:128] = down(0, 128, left, zc).astype(BF)
        send(left_out.at[i, 0:128], from_right.at[i, 0:128], g_send.at[1, i], g_recv.at[1, i], left_dev)

    def return_second(i):
        zc = out_z(i)
        mine = down(0, 128, right, zc)
        wait_bytes(far_left.at[i], f_recv.at[0, i])
        right_out[i, 0:128] = (mine + far_left[i].astype(F32)).astype(BF)
        send(right_out.at[i, 0:128], from_left.at[i, 0:128], g_send.at[0, i], g_recv.at[0, i], right_dev)
        mine = down(128, 128, left, zc)
        wait_bytes(far_right.at[i], f_recv.at[1, i])
        left_out[i, 128:256] = (mine + far_right[i].astype(F32)).astype(BF)
        send(left_out.at[i, 128:256], from_right.at[i, 128:256], g_send.at[1, i], g_recv.at[1, i], left_dev)

    def return_third(i):
        zc = out_z(i)
        mine = down(0, 256, x, zc)
        wait_bytes(from_left.at[i], g_recv.at[0, i])
        wait_bytes(from_right.at[i], g_recv.at[1, i])
        total = mine + from_left[i].astype(F32) + from_right[i].astype(F32)
        summed[i] = total.astype(BF).reshape(8, 32, 256)
        for dl in (1, 0):
            to_lo = z_lo if dl == 0 else 1 - z_lo
            for dy in (2, 1, 3, 0):
                to_y = lax.rem(y + dy, 4)
                src = summed.at[i, to_lo * 4 + to_y]
                dst = final_in.at[row, z_hi]
                if CHUNK_ORDER_OUT[i] == 0 and dl == 0 and dy == 0:
                    local_copy(src, dst, z_recv)
                else:
                    send(src, dst, z_send.at[i], z_recv, place(to_lo, to_y, zc, x, core))

    return_first(0)
    return_first(1)
    return_second(0)
    return_first(2)
    return_second(1)
    return_third(0)
    return_first(3)
    return_second(2)
    return_third(1)
    return_second(3)
    return_third(2)
    return_third(3)

    wait_bytes(final_in, z_recv)
    pieces = final_in[...].astype(F32).reshape(16, 2, 32, 256)
    expert_out = (pieces[:, 0] + pieces[:, 1]).astype(BF).reshape(512, 256)
    picked0 = dot(pick0.astype(BF), expert_out)
    picked1 = dot(pick1.astype(BF), expert_out)
    mixed = stream_v[...].astype(F32) + (gates[:, 0:1] * picked0 + gates[:, 1:2] * picked1)
    out[...] = mixed.astype(BF)

    wait_bytes(payload.at[0:15], p1_send.at[0])

    @pl.when(jnp.logical_not(p_self))
    def _():
        wait_bytes(payload.at[0], p1_send.at[1])

    wait_bytes(w_out, ws_sem.at[0])
    wait_bytes(gate_w.at[0], ws_sem.at[1])
    wait_bytes(up_w.at[0], ws_sem.at[2])
    wait_bytes(down_w.at[0], ws_sem.at[3])
    wait_bytes(heads_in.at[0], px_send.at[0])
    wait_bytes(heads_in.at[0], px_send.at[1])
    wait_bytes(heads_in.at[0, 0:2], px_send.at[2])
    wait_bytes(heads_in.at[0, 0:2], px_send.at[3])
    wait_bytes(final_in.at[0:7], rs_send.at[0])

    @pl.when(z_lo != core)
    def _():
        wait_bytes(payload.at[0:4], rs_send.at[1])

    wait_bytes(payload.at[0:7], d1_send.at[0])
    for dz in range(1, 4):
        wait_bytes(payload.at[0:8], d1_send.at[dz])
    for way in range(2):
        for i in range(4):
            wait_bytes(payload.at[0:8], d2_send.at[way, i])
            wait_bytes(payload.at[0:4], d3_send.at[way, i])
            wait_bytes(far_left.at[0], f_send.at[way, i])
            wait_bytes(from_left.at[0], g_send.at[way, i])
    wait_bytes(pre, ex_send.at[0])
    wait_bytes(squares, ex_send.at[1])
    for i in range(4):
        count = 7 if CHUNK_ORDER_OUT[i] == 0 else 8
        wait_bytes(payload.at[0:count], z_send.at[i])


def per_device(stream, heads_out, w_out, norm_gain, expert_ids, route_gates, w_gate, w_up, w_down):
    hbm = pl.BlockSpec(memory_space=pl.ANY)
    vmem = pl.BlockSpec(memory_space=pltpu.VMEM)
    dma = pltpu.SemaphoreType.DMA
    scratch = [
        pltpu.VMEM((4, 4, 4, 32, 256), BF),
        pltpu.VMEM((2, 1024, 256), BF),
        pltpu.VMEM((4, 2, 4, 32, 256), BF),
        pltpu.VMEM((8, 128, 256), BF),
        pltpu.VMEM((128, 256), BF),
        pltpu.VMEM((2, 16, 256, 256), BF),
        pltpu.VMEM((2, 16, 256, 256), BF),
        pltpu.VMEM((2, 16, 256, 256), BF),
        pltpu.VMEM((16, 32, 256), BF),
        pltpu.VMEM((4, 4, 8, 32, 256), BF),
        pltpu.VMEM((4, 256, 256), F32),
        pltpu.VMEM((4, 256, 256), F32),
        pltpu.VMEM((256, 128), F32),
        pltpu.VMEM((256, 128), F32),
        pltpu.VMEM((2, 256, 256), BF),
        pltpu.VMEM((4, 256, 256), BF),
        pltpu.VMEM((4, 256, 256), BF),
        pltpu.VMEM((4, 256, 256), BF),
        pltpu.VMEM((4, 128, 256), BF),
        pltpu.VMEM((4, 128, 256), BF),
        pltpu.VMEM((4, 256, 256), BF),
        pltpu.VMEM((4, 256, 256), BF),
        pltpu.VMEM((4, 8, 32, 256), BF),
        pltpu.VMEM((8, 4, 32, 256), BF),
        dma((1,)),
        dma((4,)),
        dma((4,)),
        dma((4,)),
        dma,
        dma((2,)),
        dma((4,)),
        dma((4,)),
        dma,
        dma((2,)),
        dma((4,)),
        dma((4,)),
        dma((2, 4)),
        dma((2, 4)),
        dma((2, 4)),
        dma((2, 4)),
        dma((2,)),
        dma((2,)),
        dma((2, 4)),
        dma((2, 4)),
        dma((2, 4)),
        dma((2, 4)),
        dma,
        dma((4,)),
    ]
    return pl.pallas_call(
        kernel,
        out_shape=jax.ShapeDtypeStruct((128, 256), BF),
        in_specs=[hbm, hbm, hbm, vmem, vmem, vmem, hbm, hbm, hbm],
        out_specs=vmem,
        scratch_shapes=scratch,
        compiler_params=pltpu.CompilerParams(
            has_side_effects=True, vmem_limit_bytes=48 * 1024 * 1024
        ),
        name="block",
    )(
        stream,
        heads_out,
        w_out,
        norm_gain.reshape(32, 1, 256),
        expert_ids,
        route_gates,
        w_gate.reshape(16, 2, 256, 256),
        w_up.reshape(16, 2, 256, 256),
        w_down,
    )


def solution(mesh):
    return jax.shard_map(
        per_device,
        mesh=mesh,
        in_specs=(
            P("row", "col"),
            P("row", "col"),
            P("row", "col"),
            P(),
            P("row", None),
            P("row", None),
            P(None, ("row", "col")),
            P(None, ("row", "col")),
            P(("row", "col"), None),
        ),
        out_specs=P("row", "col"),
        check_vma=False,
    )
```

```python
import jax
import jax.numpy as jnp
from jax import lax
from jax.experimental import pallas as pl
from jax.experimental.pallas import tpu as pltpu
from jax.sharding import PartitionSpec as P

MESH = pl.DeviceIdType.MESH
BF = jnp.bfloat16
F32 = jnp.float32
WIDTH = 8192
CHUNK_ORDER_IN = (0, 1, 3, 2)
CHUNK_ORDER_OUT = (2, 1, 3, 0)


def place(z_lo, y, z_hi, x, core):
    return (z_lo * 4 + y, z_hi * 8 + x * 2 + core)


def local_copy(src, dst, sem):
    copy = pltpu.make_async_copy(src, dst, sem)
    copy.start()


def send(src, dst, send_sem, recv_sem, device):
    copy = pltpu.make_async_remote_copy(
        src_ref=src,
        dst_ref=dst,
        send_sem=send_sem,
        recv_sem=recv_sem,
        device_id=device,
        device_id_type=MESH,
    )
    copy.start()


def wait_bytes(view, sem):
    pltpu.make_async_copy(view, view, sem).wait()


def dot(a, b):
    return jnp.dot(a, b, preferred_element_type=F32)


def kernel(
    stream, heads, w_out, gain_hbm, ids_hbm, gates_hbm, w_gate, w_up, w_down,
    out,
    heads_in, w_out_pair, proj_out, proj_in, stream_v, gate_w, up_w, down_w,
    gain, ids, gates, spread, pick, gate_col,
    payload, tokens, pre, pre_in, squares, squares_in, act,
    far_out, right_out, left_out, far_left, far_right, from_left, from_right, summed, final_in,
    in_sem, w_sem, wr_sem, ws_sem,
    p1_recv, p1_send, px_recv, px_send, rs_recv, rs_send,
    d1_recv, d1_send, d2_recv, d2_send, d3_recv, d3_send, ex_recv, ex_send,
    f_recv, f_send, g_recv, g_send, z_recv, z_send,
):
    row = lax.axis_index("row")
    col = lax.axis_index("col")
    z_lo, y = lax.div(row, 4), lax.rem(row, 4)
    z_hi = lax.div(col, 8)
    x = lax.rem(lax.div(col, 2), 4)
    core = lax.rem(col, 2)
    other = 1 - core
    right = lax.rem(x + 1, 4)
    left = lax.rem(x + 3, 4)
    far = lax.rem(x + 2, 4)
    closers = []

    def finish():
        for close in closers:
            close()

    def later(view, sem):
        closers.append(lambda: wait_bytes(view, sem))

    def later_if(condition, view, sem):
        def close():
            @pl.when(condition)
            def _():
                wait_bytes(view, sem)

        closers.append(close)

    right_dev = place(z_lo, y, z_hi, right, core)
    left_dev = place(z_lo, y, z_hi, left, core)
    pair_dev = place(z_lo, y, z_hi, x, other)

    barrier = pltpu.get_barrier_semaphore()
    p_row_lo = lax.div(z_hi, 2)
    p_row_y = lax.rem(z_hi, 2) * 2 + lax.div(x, 2)
    p_self = jnp.logical_and(jnp.logical_and(p_row_lo == z_lo, p_row_y == y), z_lo == core)
    rs_self = z_lo == core

    def greet(device):
        pl.semaphore_signal(barrier, inc=1, device_id=device, device_id_type=MESH)

    def greet_other(device):
        @pl.when(jnp.logical_or(device[0] != row, device[1] != col))
        def _():
            greet(device)

    greet(right_dev)
    greet(left_dev)
    greet(pair_dev)
    for from_y in range(4):
        for from_x in range(2):
            for from_core in range(2):
                greet_other(
                    place(core, from_y, 2 * z_lo + lax.div(y, 2), 2 * lax.rem(y, 2) + from_x, from_core)
                )
    for from_lo in range(2):
        for from_y in range(4):
            greet_other(place(from_lo, from_y, z_hi, x, z_lo))
    pl.semaphore_wait(barrier, 27 - p_self.astype(jnp.int32) - rs_self.astype(jnp.int32))

    own_group = lax.rem(x, 2) * 2 + core
    for dz in (2, 1, 3, 0):
        for dx in (2, 1, 3, 0):
            to_x = lax.rem(x + dx, 4)
            to_z = lax.rem(z_hi + dz, 4)
            src = heads.at[pl.ds(to_x * 32, 32), :]
            dst = heads_in.at[to_x, own_group, y]
            device = place(p_row_lo, p_row_y, to_z, to_x, z_lo)
            if dz == 0 and dx == 0:
                @pl.when(p_self)
                def _():
                    local_copy(src, dst, p1_recv)

                @pl.when(jnp.logical_not(p_self))
                def _():
                    send(src, dst, p1_send.at[1], p1_recv, device)
            else:
                send(src, dst, p1_send.at[0], p1_recv, device)

    later(payload.at[0:15], p1_send.at[0])
    later_if(jnp.logical_not(p_self), payload.at[0], p1_send.at[1])

    local_copy(w_out, w_out_pair.at[core], w_sem.at[0])
    send(w_out, w_out_pair.at[core], ws_sem.at[0], wr_sem.at[0], pair_dev)
    local_copy(ids_hbm, ids, in_sem.at[1])
    local_copy(gates_hbm, gates, in_sem.at[2])
    local_copy(stream, stream_v, in_sem.at[0])
    local_copy(gain_hbm, gain, in_sem.at[3])
    local_copy(w_gate.at[:, core], gate_w.at[core], w_sem.at[1])
    local_copy(w_up.at[:, core], up_w.at[core], w_sem.at[2])
    send(w_gate.at[:, other], gate_w.at[core], ws_sem.at[1], wr_sem.at[1], pair_dev)
    send(w_up.at[:, other], up_w.at[core], ws_sem.at[2], wr_sem.at[2], pair_dev)

    def load_down(b, carry):
        mine = pl.multiple_of((2 * b + core) * 256, 256)
        theirs = pl.multiple_of((2 * b + other) * 256, 256)
        local_copy(w_down.at[:, pl.ds(mine, 256)], down_w.at[core, b], w_sem.at[3])
        send(w_down.at[:, pl.ds(theirs, 256)], down_w.at[core, b], ws_sem.at[3], wr_sem.at[3], pair_dev)
        return carry

    lax.fori_loop(0, 16, load_down, 0)
    later(w_out, ws_sem.at[0])
    later(gate_w.at[0], ws_sem.at[1])
    later(up_w.at[0], ws_sem.at[2])
    later(down_w.at[0], ws_sem.at[3])

    wait_bytes(ids, in_sem.at[1])
    wait_bytes(gates, in_sem.at[2])
    expert_sub = lax.broadcasted_iota(jnp.int32, (16, 128), 0)
    lane = lax.broadcasted_iota(jnp.int32, (128, 128), 1)
    sub = lax.broadcasted_iota(jnp.int32, (128, 128), 0)
    first = (ids[0:1, :] == expert_sub).astype(F32)
    second = (ids[1:2, :] == expert_sub).astype(F32)
    earlier = dot((first + second).astype(BF), (sub < lane).astype(BF))
    slot_sub = lax.broadcasted_iota(jnp.int32, (512, 128), 0)
    slot0 = ids[0:1, :] * 32 + jnp.sum(earlier * first, axis=0, keepdims=True).astype(jnp.int32)
    slot1 = ids[1:2, :] * 32 + jnp.sum(earlier * second, axis=0, keepdims=True).astype(jnp.int32)
    match0 = (slot0 == slot_sub).astype(F32)
    match1 = (slot1 == slot_sub).astype(F32)
    spread[...] = (match0 + match1).astype(BF)
    pick[0] = match0.T.astype(BF)
    pick[1] = match1.T.astype(BF)
    for k in range(2):
        gate_col[k] = jnp.broadcast_to(gates[k:k + 1, :], (128, 128)).T
    pre[...] = jnp.zeros_like(pre)
    squares[...] = jnp.zeros_like(squares)

    def project(group):
        rows = [heads_in[group, j].reshape(128, 256) for j in range(4)]
        for dc in range(2):
            c = core if dc == 0 else other
            total = dot(rows[0], w_out_pair[c, 0:256, :])
            for j in range(1, 4):
                total = total + dot(rows[j], w_out_pair[c, j * 256:(j + 1) * 256, :])
            proj_out[group, c] = total.astype(BF).reshape(4, 32, 256)
        for dy in (2, 1, 3, 0):
            to_y = lax.rem(y + dy, 4)
            for dc in range(2):
                c = core if dc == 0 else other
                src = proj_out.at[group, c, to_y]
                dst = proj_in.at[row, pl.ds(group * 32, 32), :]
                device = place(core, to_y, z_hi, x, c)
                if dy == 0 and dc == 0:
                    @pl.when(rs_self)
                    def _():
                        local_copy(src, dst, rs_recv)

                    @pl.when(jnp.logical_not(rs_self))
                    def _():
                        send(src, dst, rs_send.at[1], rs_recv, device)
                else:
                    send(src, dst, rs_send.at[0], rs_recv, device)

    wait_bytes(heads_in.at[x], p1_recv)
    later(heads_in.at[0], px_send.at[0])
    later(heads_in.at[0], px_send.at[1])
    later(heads_in.at[0, 0:2], px_send.at[2])
    later(heads_in.at[0, 0:2], px_send.at[3])
    later(final_in.at[0:7], rs_send.at[0])
    later_if(jnp.logical_not(rs_self), payload.at[0:4], rs_send.at[1])
    send(heads_in.at[x], heads_in.at[x], px_send.at[0], px_recv.at[0], right_dev)
    send(heads_in.at[x], heads_in.at[x], px_send.at[1], px_recv.at[1], left_dev)
    wait_bytes(w_out_pair.at[core], w_sem.at[0])
    wait_bytes(w_out_pair.at[other], wr_sem.at[0])
    project(x)
    wait_bytes(heads_in.at[left], px_recv.at[0])
    send(heads_in.at[left, 0:2], heads_in.at[left, 0:2], px_send.at[2], px_recv.at[2], right_dev)
    wait_bytes(heads_in.at[right], px_recv.at[1])
    send(heads_in.at[right, 2:4], heads_in.at[right, 2:4], px_send.at[3], px_recv.at[3], left_dev)
    project(left)
    project(right)
    wait_bytes(heads_in.at[far, 0:2], px_recv.at[2])
    wait_bytes(heads_in.at[far, 2:4], px_recv.at[3])
    project(far)

    wait_bytes(stream_v, in_sem.at[0])
    wait_bytes(proj_in, rs_recv)
    residual = stream_v[...].astype(F32)
    for r in range(8):
        residual = residual + proj_in[r].astype(F32)
    stream_v[...] = residual.astype(BF)
    for dz in range(4):
        later(payload.at[0:7 if dz == 0 else 8], d1_send.at[dz])

    payload[...] = dot(spread[...], stream_v[...]).astype(BF).reshape(16, 32, 256)
    for dz in CHUNK_ORDER_IN:
        to_z = lax.rem(z_hi + dz, 4)
        for dl in (1, 0):
            to_lo = z_lo if dl == 0 else 1 - z_lo
            for dy in (2, 1, 3, 0):
                to_y = lax.rem(y + dy, 4)
                expert = 2 * (to_lo * 4 + to_y) + lax.div(to_z, 2)
                src = payload.at[expert]
                dst = tokens.at[x, z_hi, row]
                if dz == 0 and dl == 0 and dy == 0:
                    local_copy(src, dst, d1_recv.at[dz])
                else:
                    send(src, dst, d1_send.at[dz], d1_recv.at[dz], place(to_lo, to_y, to_z, x, core))

    wait_bytes(gain, in_sem.at[3])
    wait_bytes(gate_w.at[core], w_sem.at[1])
    wait_bytes(up_w.at[core], w_sem.at[2])
    wait_bytes(gate_w.at[other], wr_sem.at[1])
    wait_bytes(up_w.at[other], wr_sem.at[2])

    def absorb(from_x, from_z):
        block = tokens[from_x, from_z].reshape(256, 256).astype(F32)
        square = block * block
        squares[...] += square[:, 0:128] + square[:, 128:256]
        scaled = (block * gain[from_z * 8 + from_x * 2 + core]).astype(BF)
        b = from_z * 4 + from_x
        for c in range(2):
            pre[c] += dot(scaled, gate_w[c, b])
            pre[2 + c] += dot(scaled, up_w[c, b])

    def chunk_z(i):
        return lax.rem(z_hi + 4 - CHUNK_ORDER_IN[i], 4)

    def gather_first(i):
        zc = chunk_z(i)
        wait_bytes(tokens.at[x, zc], d1_recv.at[CHUNK_ORDER_IN[i]])
        view = tokens.at[x, zc]
        send(view, view, d2_send.at[0, i], d2_recv.at[0, i], right_dev)
        send(view, view, d2_send.at[1, i], d2_recv.at[1, i], left_dev)
        absorb(x, zc)

    def gather_second(i):
        zc = chunk_z(i)
        wait_bytes(tokens.at[left, zc], d2_recv.at[0, i])
        view = tokens.at[left, zc, 0:4]
        send(view, view, d3_send.at[0, i], d3_recv.at[0, i], right_dev)
        wait_bytes(tokens.at[right, zc], d2_recv.at[1, i])
        view = tokens.at[right, zc, 4:8]
        send(view, view, d3_send.at[1, i], d3_recv.at[1, i], left_dev)
        absorb(left, zc)
        absorb(right, zc)

    def gather_third(i):
        zc = chunk_z(i)
        wait_bytes(tokens.at[far, zc, 0:4], d3_recv.at[0, i])
        wait_bytes(tokens.at[far, zc, 4:8], d3_recv.at[1, i])
        absorb(far, zc)

    for way in range(2):
        for i in range(4):
            later(payload.at[0:8], d2_send.at[way, i])
            later(payload.at[0:4], d3_send.at[way, i])
    for i in range(6):
        if i < 4:
            gather_first(i)
        if 1 <= i < 5:
            gather_second(i - 1)
        if i >= 2:
            gather_third(i - 2)

    later(pre, ex_send.at[0])
    later(squares, ex_send.at[1])

    send(pre, pre_in, ex_send.at[0], ex_recv.at[0], pair_dev)
    send(squares, squares_in, ex_send.at[1], ex_recv.at[1], pair_dev)
    wait_bytes(squares_in, ex_recv.at[1])
    wait_bytes(pre_in, ex_recv.at[0])
    mean = jnp.sum(squares[...] + squares_in[...], axis=1, keepdims=True) / WIDTH
    scale = lax.rsqrt(mean + 1e-05)
    for c in range(2):
        gate_pre = (pre[c] + pre_in[c]) * scale
        up_pre = (pre[2 + c] + pre_in[2 + c]) * scale
        act[c] = (gate_pre / (1.0 + jnp.exp(-gate_pre)) * up_pre).astype(BF)

    wait_bytes(down_w.at[core], w_sem.at[3])
    wait_bytes(down_w.at[other], wr_sem.at[3])

    def down(start, rows, to_x, zc):
        b = zc * 4 + to_x
        return dot(act[0, start:start + rows, :], down_w[0, b]) + dot(
            act[1, start:start + rows, :], down_w[1, b]
        )

    def out_z(i):
        return lax.rem(z_hi + CHUNK_ORDER_OUT[i], 4)

    def return_first(i):
        zc = out_z(i)
        far_out[i] = down(0, 256, far, zc).astype(BF)
        send(far_out.at[i, 0:128], far_left.at[i], f_send.at[0, i], f_recv.at[0, i], right_dev)
        send(far_out.at[i, 128:256], far_right.at[i], f_send.at[1, i], f_recv.at[1, i], left_dev)
        right_out[i, 128:256] = down(128, 128, right, zc).astype(BF)
        send(right_out.at[i, 128:256], from_left.at[i, 128:256], g_send.at[0, i], g_recv.at[0, i], right_dev)
        left_out[i, 0:128] = down(0, 128, left, zc).astype(BF)
        send(left_out.at[i, 0:128], from_right.at[i, 0:128], g_send.at[1, i], g_recv.at[1, i], left_dev)

    def return_second(i):
        zc = out_z(i)
        mine = down(0, 128, right, zc)
        wait_bytes(far_left.at[i], f_recv.at[0, i])
        right_out[i, 0:128] = (mine + far_left[i].astype(F32)).astype(BF)
        send(right_out.at[i, 0:128], from_left.at[i, 0:128], g_send.at[0, i], g_recv.at[0, i], right_dev)
        mine = down(128, 128, left, zc)
        wait_bytes(far_right.at[i], f_recv.at[1, i])
        left_out[i, 128:256] = (mine + far_right[i].astype(F32)).astype(BF)
        send(left_out.at[i, 128:256], from_right.at[i, 128:256], g_send.at[1, i], g_recv.at[1, i], left_dev)

    def return_third(i):
        zc = out_z(i)
        mine = down(0, 256, x, zc)
        wait_bytes(from_left.at[i], g_recv.at[0, i])
        wait_bytes(from_right.at[i], g_recv.at[1, i])
        total = mine + from_left[i].astype(F32) + from_right[i].astype(F32)
        summed[i] = total.astype(BF).reshape(8, 32, 256)
        for dl in (1, 0):
            to_lo = z_lo if dl == 0 else 1 - z_lo
            for dy in (2, 1, 3, 0):
                to_y = lax.rem(y + dy, 4)
                src = summed.at[i, to_lo * 4 + to_y]
                dst = final_in.at[row, z_hi]
                if CHUNK_ORDER_OUT[i] == 0 and dl == 0 and dy == 0:
                    local_copy(src, dst, z_recv)
                else:
                    send(src, dst, z_send.at[i], z_recv, place(to_lo, to_y, zc, x, core))

    for way in range(2):
        for i in range(4):
            later(far_left.at[0], f_send.at[way, i])
            later(from_left.at[0], g_send.at[way, i])
    for i in range(4):
        later(payload.at[0:7 if CHUNK_ORDER_OUT[i] == 0 else 8], z_send.at[i])
    return_first(0)
    return_first(1)
    return_second(0)
    return_first(2)
    return_second(1)
    return_third(0)
    return_first(3)
    return_second(2)
    return_third(1)
    return_second(3)
    return_third(2)
    return_third(3)

    wait_bytes(final_in, z_recv)
    pieces = final_in[...].astype(F32).reshape(16, 2, 32, 256)
    expert_out = (pieces[:, 0] + pieces[:, 1]).astype(BF).reshape(512, 256)
    picked0 = dot(pick[0], expert_out)
    picked1 = dot(pick[1], expert_out)
    mixed = stream_v[...].astype(F32) + (
        gate_col[0, :, 0:1] * picked0 + gate_col[1, :, 0:1] * picked1
    )
    out[...] = mixed.astype(BF)
    finish()


def per_device(stream, heads_out, w_out, norm_gain, expert_ids, route_gates, w_gate, w_up, w_down):
    hbm = pl.BlockSpec(memory_space=pl.ANY)
    vmem = pl.BlockSpec(memory_space=pltpu.VMEM)
    dma = pltpu.SemaphoreType.DMA
    scratch = [
        pltpu.VMEM((4, 4, 4, 32, 256), BF),
        pltpu.VMEM((2, 1024, 256), BF),
        pltpu.VMEM((4, 2, 4, 32, 256), BF),
        pltpu.VMEM((8, 128, 256), BF),
        pltpu.VMEM((128, 256), BF),
        pltpu.VMEM((2, 16, 256, 256), BF),
        pltpu.VMEM((2, 16, 256, 256), BF),
        pltpu.VMEM((2, 16, 256, 256), BF),
        pltpu.VMEM((32, 1, 256), F32),
        pltpu.VMEM((2, 128), jnp.int32),
        pltpu.VMEM((2, 128), F32),
        pltpu.VMEM((512, 128), BF),
        pltpu.VMEM((2, 128, 512), BF),
        pltpu.VMEM((2, 128, 128), F32),
        pltpu.VMEM((16, 32, 256), BF),
        pltpu.VMEM((4, 4, 8, 32, 256), BF),
        pltpu.VMEM((4, 256, 256), F32),
        pltpu.VMEM((4, 256, 256), F32),
        pltpu.VMEM((256, 128), F32),
        pltpu.VMEM((256, 128), F32),
        pltpu.VMEM((2, 256, 256), BF),
        pltpu.VMEM((4, 256, 256), BF),
        pltpu.VMEM((4, 256, 256), BF),
        pltpu.VMEM((4, 256, 256), BF),
        pltpu.VMEM((4, 128, 256), BF),
        pltpu.VMEM((4, 128, 256), BF),
        pltpu.VMEM((4, 256, 256), BF),
        pltpu.VMEM((4, 256, 256), BF),
        pltpu.VMEM((4, 8, 32, 256), BF),
        pltpu.VMEM((8, 4, 32, 256), BF),
        dma((4,)),
        dma((4,)),
        dma((4,)),
        dma((4,)),
        dma,
        dma((2,)),
        dma((4,)),
        dma((4,)),
        dma,
        dma((2,)),
        dma((4,)),
        dma((4,)),
        dma((2, 4)),
        dma((2, 4)),
        dma((2, 4)),
        dma((2, 4)),
        dma((2,)),
        dma((2,)),
        dma((2, 4)),
        dma((2, 4)),
        dma((2, 4)),
        dma((2, 4)),
        dma,
        dma((4,)),
    ]
    return pl.pallas_call(
        kernel,
        out_shape=jax.ShapeDtypeStruct((128, 256), BF),
        in_specs=[hbm] * 9,
        out_specs=vmem,
        scratch_shapes=scratch,
        compiler_params=pltpu.CompilerParams(
            collective_id=0, has_side_effects=True, vmem_limit_bytes=60 * 1024 * 1024
        ),
        name="block",
    )(
        stream,
        heads_out,
        w_out,
        norm_gain.reshape(32, 1, 256),
        expert_ids.T,
        route_gates.T,
        w_gate.reshape(16, 2, 256, 256),
        w_up.reshape(16, 2, 256, 256),
        w_down,
    )


def solution(mesh):
    return jax.shard_map(
        per_device,
        mesh=mesh,
        in_specs=(
            P("row", "col"),
            P("row", "col"),
            P("row", "col"),
            P(),
            P("row", None),
            P("row", None),
            P(None, ("row", "col")),
            P(None, ("row", "col")),
            P(("row", "col"), None),
        ),
        out_specs=P("row", "col"),
        check_vma=False,
    )
```

```python
import jax
import jax.numpy as jnp
from jax import lax
from jax.experimental import pallas as pl
from jax.experimental.pallas import tpu as pltpu
from jax.sharding import PartitionSpec as P

MESH = pl.DeviceIdType.MESH
BF = jnp.bfloat16
F32 = jnp.float32
WIDTH = 8192
CHUNK_ORDER_IN = (0, 1, 3, 2)
CHUNK_ORDER_OUT = (2, 1, 3, 0)
Y_STEPS = ((1, 3), (0, 2))
PARTS = len(Y_STEPS)
BLOCKS = tuple(2 * len(part) for part in Y_STEPS)
MOST = max(BLOCKS)
PLAN = (
    (
        "d00", "d01", "d03", "d02",
    ),
    (
        "p00", "p01", "p02", "p03", "d10", "d11", "d13", "d12", "q00", "q01", "q02", "q03",
        "r00", "r01", "r02", "r03", "e0", "p10", "p11", "p12", "p13", "q10", "q11", "q12",
        "q13", "f0",
    ),
    (
        "a00", "a01", "a02", "a03", "r10", "r11", "r12", "r13", "e1", "b00", "b01", "b02",
        "b03", "f1", "a10", "a11", "c00", "c01", "b10", "a12", "b11", "a13", "c02", "c03",
        "c10", "b12", "c11", "b13", "c12", "c13",
    ),
)


def place(z_lo, y, z_hi, x, core):
    return (z_lo * 4 + y, z_hi * 8 + x * 2 + core)


def local_copy(src, dst, sem):
    copy = pltpu.make_async_copy(src, dst, sem)
    copy.start()


def send(src, dst, send_sem, recv_sem, device):
    copy = pltpu.make_async_remote_copy(
        src_ref=src,
        dst_ref=dst,
        send_sem=send_sem,
        recv_sem=recv_sem,
        device_id=device,
        device_id_type=MESH,
    )
    copy.start()


def wait_bytes(view, sem):
    pltpu.make_async_copy(view, view, sem).wait()


def dot(a, b):
    return jnp.dot(a, b, preferred_element_type=F32)


def kernel(
    stream, heads, w_out, gain_hbm, ids_hbm, gates_hbm, w_gate, w_up, w_down,
    out,
    heads_in, w_out_pair, proj_out, proj_in, stream_v, gate_w, up_w, down_w,
    gain, ids, gates, spread, pick, gate_col,
    payload, tokens, pre, pre_in, squares, squares_in, act,
    far_out, right_out, left_out, kept, far_left, far_right, from_left, from_right, summed, final_in,
    in_sem, w_sem, wr_sem, ws_sem,
    p1_recv, p1_send, px_recv, px_send, rs_recv, rs_send,
    d1_recv, d1_send, d2_recv, d2_send, d3_recv, d3_send, ex_recv, ex_send,
    f_recv, f_send, g_recv, g_send, z_recv, z_send,
):
    row = lax.axis_index("row")
    col = lax.axis_index("col")
    z_lo, y = lax.div(row, 4), lax.rem(row, 4)
    z_hi = lax.div(col, 8)
    x = lax.rem(lax.div(col, 2), 4)
    core = lax.rem(col, 2)
    other = 1 - core
    right = lax.rem(x + 1, 4)
    left = lax.rem(x + 3, 4)
    far = lax.rem(x + 2, 4)
    closers = []

    def finish():
        for close in closers:
            close()

    def later(view, sem):
        closers.append(lambda: wait_bytes(view, sem))

    def later_if(condition, view, sem):
        def close():
            @pl.when(condition)
            def _():
                wait_bytes(view, sem)

        closers.append(close)

    right_dev = place(z_lo, y, z_hi, right, core)
    left_dev = place(z_lo, y, z_hi, left, core)
    pair_dev = place(z_lo, y, z_hi, x, other)

    barrier = pltpu.get_barrier_semaphore()
    p_row_lo = lax.div(z_hi, 2)
    p_row_y = lax.rem(z_hi, 2) * 2 + lax.div(x, 2)
    p_self = jnp.logical_and(jnp.logical_and(p_row_lo == z_lo, p_row_y == y), z_lo == core)
    rs_self = z_lo == core

    def greet(device):
        pl.semaphore_signal(barrier, inc=1, device_id=device, device_id_type=MESH)

    def greet_other(device):
        @pl.when(jnp.logical_or(device[0] != row, device[1] != col))
        def _():
            greet(device)

    greet(right_dev)
    greet(left_dev)
    greet(pair_dev)
    for from_y in range(4):
        for from_x in range(2):
            for from_core in range(2):
                greet_other(
                    place(core, from_y, 2 * z_lo + lax.div(y, 2), 2 * lax.rem(y, 2) + from_x, from_core)
                )
    for from_lo in range(2):
        for from_y in range(4):
            greet_other(place(from_lo, from_y, z_hi, x, z_lo))
    pl.semaphore_wait(barrier, 27 - p_self.astype(jnp.int32) - rs_self.astype(jnp.int32))

    own_group = lax.rem(x, 2) * 2 + core
    for dz in (2, 1, 3, 0):
        for dx in (2, 1, 3, 0):
            to_x = lax.rem(x + dx, 4)
            to_z = lax.rem(z_hi + dz, 4)
            src = heads.at[pl.ds(to_x * 32, 32), :]
            dst = heads_in.at[to_x, own_group, y]
            device = place(p_row_lo, p_row_y, to_z, to_x, z_lo)
            if dz == 0 and dx == 0:
                @pl.when(p_self)
                def _():
                    local_copy(src, dst, p1_recv)

                @pl.when(jnp.logical_not(p_self))
                def _():
                    send(src, dst, p1_send.at[1], p1_recv, device)
            else:
                send(src, dst, p1_send.at[0], p1_recv, device)

    later(payload.at[0:15], p1_send.at[0])
    later_if(jnp.logical_not(p_self), payload.at[0], p1_send.at[1])

    local_copy(w_out, w_out_pair.at[core], w_sem.at[0])
    send(w_out, w_out_pair.at[core], ws_sem.at[0], wr_sem.at[0], pair_dev)
    local_copy(ids_hbm, ids, in_sem.at[1])
    local_copy(gates_hbm, gates, in_sem.at[2])
    local_copy(stream, stream_v, in_sem.at[0])
    local_copy(gain_hbm, gain, in_sem.at[3])
    local_copy(w_gate.at[:, core], gate_w.at[core], w_sem.at[1])
    local_copy(w_up.at[:, core], up_w.at[core], w_sem.at[2])
    send(w_gate.at[:, other], gate_w.at[core], ws_sem.at[1], wr_sem.at[1], pair_dev)
    send(w_up.at[:, other], up_w.at[core], ws_sem.at[2], wr_sem.at[2], pair_dev)

    def load_down(b, carry):
        mine = pl.multiple_of((2 * b + core) * 256, 256)
        theirs = pl.multiple_of((2 * b + other) * 256, 256)
        local_copy(w_down.at[:, pl.ds(mine, 256)], down_w.at[core, b], w_sem.at[3])
        send(w_down.at[:, pl.ds(theirs, 256)], down_w.at[core, b], ws_sem.at[3], wr_sem.at[3], pair_dev)
        return carry

    lax.fori_loop(0, 16, load_down, 0)
    later(w_out, ws_sem.at[0])
    later(gate_w.at[0], ws_sem.at[1])
    later(up_w.at[0], ws_sem.at[2])
    later(down_w.at[0], ws_sem.at[3])

    wait_bytes(ids, in_sem.at[1])
    wait_bytes(gates, in_sem.at[2])
    expert_sub = lax.broadcasted_iota(jnp.int32, (16, 128), 0)
    lane = lax.broadcasted_iota(jnp.int32, (128, 128), 1)
    sub = lax.broadcasted_iota(jnp.int32, (128, 128), 0)
    first = (ids[0:1, :] == expert_sub).astype(F32)
    second = (ids[1:2, :] == expert_sub).astype(F32)
    earlier = dot((first + second).astype(BF), (sub < lane).astype(BF))
    slot_sub = lax.broadcasted_iota(jnp.int32, (512, 128), 0)
    slot0 = ids[0:1, :] * 32 + jnp.sum(earlier * first, axis=0, keepdims=True).astype(jnp.int32)
    slot1 = ids[1:2, :] * 32 + jnp.sum(earlier * second, axis=0, keepdims=True).astype(jnp.int32)
    match0 = (slot0 == slot_sub).astype(F32)
    match1 = (slot1 == slot_sub).astype(F32)
    spread[...] = (match0 + match1).astype(BF)
    pick[0] = match0.T.astype(BF)
    pick[1] = match1.T.astype(BF)
    for k in range(2):
        gate_col[k] = jnp.broadcast_to(gates[k:k + 1, :], (128, 128)).T
    pre[...] = jnp.zeros_like(pre)
    squares[...] = jnp.zeros_like(squares)

    def project(group):
        rows = [heads_in[group, j].reshape(128, 256) for j in range(4)]
        for dc in range(2):
            c = core if dc == 0 else other
            total = dot(rows[0], w_out_pair[c, 0:256, :])
            for j in range(1, 4):
                total = total + dot(rows[j], w_out_pair[c, j * 256:(j + 1) * 256, :])
            proj_out[group, c] = total.astype(BF).reshape(4, 32, 256)
        for dy in (2, 1, 3, 0):
            to_y = lax.rem(y + dy, 4)
            for dc in range(2):
                c = core if dc == 0 else other
                src = proj_out.at[group, c, to_y]
                dst = proj_in.at[row, pl.ds(group * 32, 32), :]
                device = place(core, to_y, z_hi, x, c)
                if dy == 0 and dc == 0:
                    @pl.when(rs_self)
                    def _():
                        local_copy(src, dst, rs_recv)

                    @pl.when(jnp.logical_not(rs_self))
                    def _():
                        send(src, dst, rs_send.at[1], rs_recv, device)
                else:
                    send(src, dst, rs_send.at[0], rs_recv, device)

    wait_bytes(heads_in.at[x], p1_recv)
    later(final_in.at[0:7], rs_send.at[0])
    later_if(jnp.logical_not(rs_self), payload.at[0:4], rs_send.at[1])
    ends = (heads_in.at[x, 0:2], heads_in.at[x, 2:4])
    for k in range(2):
        send(ends[k], ends[k], px_send.at[0, k], px_recv.at[0, k], right_dev)
        send(ends[1 - k], ends[1 - k], px_send.at[1, k], px_recv.at[1, k], left_dev)
    wait_bytes(w_out_pair.at[core], w_sem.at[0])
    wait_bytes(w_out_pair.at[other], wr_sem.at[0])
    project(x)
    view = heads_in.at[left, 0:2]
    wait_bytes(view, px_recv.at[0, 0])
    send(view, view, px_send.at[0, 2], px_recv.at[0, 2], right_dev)
    view = heads_in.at[right, 2:4]
    wait_bytes(view, px_recv.at[1, 0])
    send(view, view, px_send.at[1, 2], px_recv.at[1, 2], left_dev)
    for way in range(2):
        for k in range(3):
            later(heads_in.at[0, 0:2], px_send.at[way, k])
    wait_bytes(heads_in.at[left, 2:4], px_recv.at[0, 1])
    project(left)
    wait_bytes(heads_in.at[right, 0:2], px_recv.at[1, 1])
    project(right)
    wait_bytes(heads_in.at[far, 0:2], px_recv.at[0, 2])
    wait_bytes(heads_in.at[far, 2:4], px_recv.at[1, 2])
    project(far)

    wait_bytes(stream_v, in_sem.at[0])
    wait_bytes(proj_in, rs_recv)
    residual = stream_v[...].astype(F32)
    for r in range(8):
        residual = residual + proj_in[r].astype(F32)
    stream_v[...] = residual.astype(BF)
    payload[...] = dot(spread[...], stream_v[...]).astype(BF).reshape(16, 32, 256)

    def dispatch(h, dz):
        to_z = lax.rem(z_hi + dz, 4)
        for step, dy in enumerate(Y_STEPS[h]):
            to_y = lax.rem(y + dy, 4)
            for dl in (1, 0):
                to_lo = z_lo if dl == 0 else 1 - z_lo
                expert = 2 * (to_lo * 4 + to_y) + lax.div(to_z, 2)
                src = payload.at[expert]
                dst = tokens.at[h, x, z_hi, step * 2 + z_lo]
                if dz == 0 and dl == 0 and dy == 0:
                    local_copy(src, dst, d1_recv.at[h, dz])
                else:
                    send(src, dst, d1_send.at[h, dz], d1_recv.at[h, dz], place(to_lo, to_y, to_z, x, core))
        later(payload.at[0:BLOCKS[h] - (dz == 0 and 0 in Y_STEPS[h])], d1_send.at[h, dz])

    def absorb(h, from_x, from_z):
        n = BLOCKS[h] * 32
        block = tokens[h, from_x, from_z, 0:BLOCKS[h]].reshape(n, 256).astype(F32)
        square = block * block
        squares[h, 0:n] += square[:, 0:128] + square[:, 128:256]
        scaled = (block * gain[from_z * 8 + from_x * 2 + core]).astype(BF)
        b = from_z * 4 + from_x
        for c in range(2):
            pre[h, c, 0:n] += dot(scaled, gate_w[c, b])
            pre[h, 2 + c, 0:n] += dot(scaled, up_w[c, b])

    def chunk_z(i):
        return lax.rem(z_hi + 4 - CHUNK_ORDER_IN[i], 4)

    def gather_first(h, i):
        zc = chunk_z(i)
        n = BLOCKS[h]
        wait_bytes(tokens.at[h, x, zc, 0:n], d1_recv.at[h, CHUNK_ORDER_IN[i]])
        ends = (tokens.at[h, x, zc, 0:n // 2], tokens.at[h, x, zc, n // 2:n])
        for k in range(2):
            send(ends[k], ends[k], d2_send.at[h, 0, i, k], d2_recv.at[h, 0, i, k], right_dev)
            send(ends[1 - k], ends[1 - k], d2_send.at[h, 1, i, k], d2_recv.at[h, 1, i, k], left_dev)
            for way in range(2):
                later(payload.at[0:n // 2], d2_send.at[h, way, i, k])
        absorb(h, x, zc)

    def gather_second(h, i):
        zc = chunk_z(i)
        n = BLOCKS[h]
        view = tokens.at[h, left, zc, 0:n // 2]
        wait_bytes(view, d2_recv.at[h, 0, i, 0])
        send(view, view, d3_send.at[h, 0, i], d3_recv.at[h, 0, i], right_dev)
        view = tokens.at[h, right, zc, n // 2:n]
        wait_bytes(view, d2_recv.at[h, 1, i, 0])
        send(view, view, d3_send.at[h, 1, i], d3_recv.at[h, 1, i], left_dev)
        for way in range(2):
            later(payload.at[0:n // 2], d3_send.at[h, way, i])
        wait_bytes(tokens.at[h, left, zc, n // 2:n], d2_recv.at[h, 0, i, 1])
        absorb(h, left, zc)
        wait_bytes(tokens.at[h, right, zc, 0:n // 2], d2_recv.at[h, 1, i, 1])
        absorb(h, right, zc)

    def gather_third(h, i):
        zc = chunk_z(i)
        n = BLOCKS[h]
        wait_bytes(tokens.at[h, far, zc, 0:n // 2], d3_recv.at[h, 0, i])
        wait_bytes(tokens.at[h, far, zc, n // 2:n], d3_recv.at[h, 1, i])
        absorb(h, far, zc)

    def exchange_first(h):
        n = BLOCKS[h] * 32
        sent, landed = pre.at[h, :, 0:n], pre_in.at[h, :, 0:n]
        send(sent, landed, ex_send.at[h, 0], ex_recv.at[h, 0], pair_dev)
        later(sent, ex_send.at[h, 0])
        sent, landed = squares.at[h, 0:n], squares_in.at[h, 0:n]
        send(sent, landed, ex_send.at[h, 1], ex_recv.at[h, 1], pair_dev)
        later(sent, ex_send.at[h, 1])

    def exchange_second(h):
        n = BLOCKS[h] * 32
        wait_bytes(squares_in.at[h, 0:n], ex_recv.at[h, 1])
        wait_bytes(pre_in.at[h, :, 0:n], ex_recv.at[h, 0])
        mean = jnp.sum(squares[h, 0:n] + squares_in[h, 0:n], axis=1, keepdims=True) / WIDTH
        scale = lax.rsqrt(mean + 1e-05)
        for c in range(2):
            gate_pre = (pre[h, c, 0:n] + pre_in[h, c, 0:n]) * scale
            up_pre = (pre[h, 2 + c, 0:n] + pre_in[h, 2 + c, 0:n]) * scale
            act[h, c, 0:n] = (gate_pre / (1.0 + jnp.exp(-gate_pre)) * up_pre).astype(BF)

    def down(h, to_x, zc):
        b = zc * 4 + to_x
        n = BLOCKS[h] * 32
        return dot(act[h, 0, 0:n], down_w[0, b]) + dot(act[h, 1, 0:n], down_w[1, b])

    def out_z(i):
        return lax.rem(z_hi + CHUNK_ORDER_OUT[i], 4)

    def return_first(h, i):
        zc = out_z(i)
        n = BLOCKS[h] * 32
        m = n // 2
        far_out[h, i, 0:n] = down(h, far, zc).astype(BF)
        send(far_out.at[h, i, 0:m], far_left.at[h, i, 0:m], f_send.at[h, 0, i], f_recv.at[h, 0, i], right_dev)
        send(far_out.at[h, i, m:n], far_right.at[h, i, 0:m], f_send.at[h, 1, i], f_recv.at[h, 1, i], left_dev)
        mine = down(h, right, zc)
        right_out[h, i, m:n] = mine[m:n].astype(BF)
        send(right_out.at[h, i, m:n], from_left.at[h, i, m:n], g_send.at[h, 0, i], g_recv.at[h, 0, i], right_dev)
        kept[h, i, 0, 0:m] = mine[0:m]
        mine = down(h, left, zc)
        left_out[h, i, 0:m] = mine[0:m].astype(BF)
        send(left_out.at[h, i, 0:m], from_right.at[h, i, 0:m], g_send.at[h, 1, i], g_recv.at[h, 1, i], left_dev)
        kept[h, i, 1, 0:m] = mine[m:n]
        for way in range(2):
            later(far_left.at[h, i, 0:m], f_send.at[h, way, i])

    def return_second(h, i):
        n = BLOCKS[h] * 32
        m = n // 2
        wait_bytes(far_left.at[h, i, 0:m], f_recv.at[h, 0, i])
        right_out[h, i, 0:m] = (kept[h, i, 0, 0:m] + far_left[h, i, 0:m].astype(F32)).astype(BF)
        send(right_out.at[h, i, 0:m], from_left.at[h, i, 0:m], g_send.at[h, 0, i], g_recv.at[h, 0, i], right_dev)
        wait_bytes(far_right.at[h, i, 0:m], f_recv.at[h, 1, i])
        left_out[h, i, m:n] = (kept[h, i, 1, 0:m] + far_right[h, i, 0:m].astype(F32)).astype(BF)
        send(left_out.at[h, i, m:n], from_right.at[h, i, m:n], g_send.at[h, 1, i], g_recv.at[h, 1, i], left_dev)
        for way in range(2):
            later(from_left.at[h, i, 0:n], g_send.at[h, way, i])

    def return_third(h, i):
        zc = out_z(i)
        n = BLOCKS[h] * 32
        mine = down(h, x, zc)
        wait_bytes(from_left.at[h, i, 0:n], g_recv.at[h, 0, i])
        wait_bytes(from_right.at[h, i, 0:n], g_recv.at[h, 1, i])
        total = mine + from_left[h, i, 0:n].astype(F32) + from_right[h, i, 0:n].astype(F32)
        summed[h, i, 0:BLOCKS[h]] = total.astype(BF).reshape(BLOCKS[h], 32, 256)
        near = CHUNK_ORDER_OUT[i] == 0
        for step, dy in enumerate(Y_STEPS[h]):
            to_y = lax.rem(y + 4 - dy, 4)
            for dl in (1, 0):
                to_lo = z_lo if dl == 0 else 1 - z_lo
                src = summed.at[h, i, step * 2 + to_lo]
                dst = final_in.at[row, z_hi]
                if near and dl == 0 and dy == 0:
                    local_copy(src, dst, z_recv)
                else:
                    send(src, dst, z_send.at[h, i], z_recv, place(to_lo, to_y, zc, x, core))
        later(payload.at[0:BLOCKS[h] - (near and 0 in Y_STEPS[h])], z_send.at[h, i])

    def wait_gate_up():
        wait_bytes(gain, in_sem.at[3])
        wait_bytes(gate_w.at[core], w_sem.at[1])
        wait_bytes(up_w.at[core], w_sem.at[2])
        wait_bytes(gate_w.at[other], wr_sem.at[1])
        wait_bytes(up_w.at[other], wr_sem.at[2])

    def wait_down():
        wait_bytes(down_w.at[core], w_sem.at[3])
        wait_bytes(down_w.at[other], wr_sem.at[3])

    steps = dict(
        d=dispatch, p=gather_first, q=gather_second, r=gather_third, e=exchange_first, f=exchange_second,
        a=return_first, b=return_second, c=return_third,
    )
    for part in PLAN:
        for name in part:
            step, h = steps[name[0]], int(name[1])
            if name[0] in "ef":
                step(h)
            else:
                step(h, int(name[2]))
        if part is PLAN[0]:
            wait_gate_up()
        if part is PLAN[1]:
            wait_down()

    wait_bytes(final_in, z_recv)
    pieces = final_in[...].astype(F32).reshape(16, 2, 32, 256)
    expert_out = (pieces[:, 0] + pieces[:, 1]).astype(BF).reshape(512, 256)
    picked0 = dot(pick[0], expert_out)
    picked1 = dot(pick[1], expert_out)
    mixed = stream_v[...].astype(F32) + (
        gate_col[0, :, 0:1] * picked0 + gate_col[1, :, 0:1] * picked1
    )
    out[...] = mixed.astype(BF)
    finish()


def per_device(stream, heads_out, w_out, norm_gain, expert_ids, route_gates, w_gate, w_up, w_down):
    hbm = pl.BlockSpec(memory_space=pl.ANY)
    vmem = pl.BlockSpec(memory_space=pltpu.VMEM)
    dma = pltpu.SemaphoreType.DMA
    scratch = [
        pltpu.VMEM((4, 4, 4, 32, 256), BF),
        pltpu.VMEM((2, 1024, 256), BF),
        pltpu.VMEM((4, 2, 4, 32, 256), BF),
        pltpu.VMEM((8, 128, 256), BF),
        pltpu.VMEM((128, 256), BF),
        pltpu.VMEM((2, 16, 256, 256), BF),
        pltpu.VMEM((2, 16, 256, 256), BF),
        pltpu.VMEM((2, 16, 256, 256), BF),
        pltpu.VMEM((32, 1, 256), F32),
        pltpu.VMEM((2, 128), jnp.int32),
        pltpu.VMEM((2, 128), F32),
        pltpu.VMEM((512, 128), BF),
        pltpu.VMEM((2, 128, 512), BF),
        pltpu.VMEM((2, 128, 128), F32),
        pltpu.VMEM((16, 32, 256), BF),
        pltpu.VMEM((PARTS, 4, 4, MOST, 32, 256), BF),
        pltpu.VMEM((PARTS, 4, MOST * 32, 256), F32),
        pltpu.VMEM((PARTS, 4, MOST * 32, 256), F32),
        pltpu.VMEM((PARTS, MOST * 32, 128), F32),
        pltpu.VMEM((PARTS, MOST * 32, 128), F32),
        pltpu.VMEM((PARTS, 2, MOST * 32, 256), BF),
        pltpu.VMEM((PARTS, 4, MOST * 32, 256), BF),
        pltpu.VMEM((PARTS, 4, MOST * 32, 256), BF),
        pltpu.VMEM((PARTS, 4, MOST * 32, 256), BF),
        pltpu.VMEM((PARTS, 4, 2, MOST * 16, 256), F32),
        pltpu.VMEM((PARTS, 4, MOST * 16, 256), BF),
        pltpu.VMEM((PARTS, 4, MOST * 16, 256), BF),
        pltpu.VMEM((PARTS, 4, MOST * 32, 256), BF),
        pltpu.VMEM((PARTS, 4, MOST * 32, 256), BF),
        pltpu.VMEM((PARTS, 4, MOST, 32, 256), BF),
        pltpu.VMEM((8, 4, 32, 256), BF),
        dma((4,)),
        dma((4,)),
        dma((4,)),
        dma((4,)),
        dma,
        dma((2,)),
        dma((2, 3)),
        dma((2, 3)),
        dma,
        dma((2,)),
        dma((PARTS, 4)),
        dma((PARTS, 4)),
        dma((PARTS, 2, 4, 2)),
        dma((PARTS, 2, 4, 2)),
        dma((PARTS, 2, 4)),
        dma((PARTS, 2, 4)),
        dma((PARTS, 2)),
        dma((PARTS, 2)),
        dma((PARTS, 2, 4)),
        dma((PARTS, 2, 4)),
        dma((PARTS, 2, 4)),
        dma((PARTS, 2, 4)),
        dma,
        dma((PARTS, 4)),
    ]
    return pl.pallas_call(
        kernel,
        out_shape=jax.ShapeDtypeStruct((128, 256), BF),
        in_specs=[hbm] * 9,
        out_specs=vmem,
        scratch_shapes=scratch,
        compiler_params=pltpu.CompilerParams(
            collective_id=0, has_side_effects=True, vmem_limit_bytes=60 * 1024 * 1024
        ),
        name="block",
    )(
        stream,
        heads_out,
        w_out,
        norm_gain.reshape(32, 1, 256),
        expert_ids.T,
        route_gates.T,
        w_gate.reshape(16, 2, 256, 256),
        w_up.reshape(16, 2, 256, 256),
        w_down,
    )


def solution(mesh):
    return jax.shard_map(
        per_device,
        mesh=mesh,
        in_specs=(
            P("row", "col"),
            P("row", "col"),
            P("row", "col"),
            P(),
            P("row", None),
            P("row", None),
            P(None, ("row", "col")),
            P(None, ("row", "col")),
            P(("row", "col"), None),
        ),
        out_specs=P("row", "col"),
        check_vma=False,
    )
```

```python
import jax
import jax.numpy as jnp
from jax import lax
from jax.experimental import pallas as pl
from jax.experimental.pallas import tpu as pltpu
from jax.sharding import PartitionSpec as P

MESH = pl.DeviceIdType.MESH
BF = jnp.bfloat16
F32 = jnp.float32
WIDTH = 8192
CHUNK_ORDER_IN = (0, 1, 3, 2)
CHUNK_ORDER_OUT = (2, 1, 3, 0)
Y_STEPS = ((0, 2), (1, 3))
PARTS = len(Y_STEPS)
BLOCKS = tuple(2 * len(part) for part in Y_STEPS)
MOST = max(BLOCKS)
PLAN = (
    (
        "d00", "d01", "d03", "d02",
    ),
    (
        "p00", "p01", "p02", "d10", "p03", "d11", "d13", "d12", "q00", "q01", "q02", "q03",
        "r00", "r01", "r02", "r03", "e0", "p10", "p11", "p12", "p13", "q10", "q11", "q12",
        "q13", "f0",
    ),
    (
        "a00", "a01", "a02", "a03", "r10", "r11", "r12", "r13", "e1", "b00", "b01", "b02",
        "b03", "f1", "a10", "a11", "c00", "c01", "b10", "a12", "b11", "a13", "c02", "c03",
        "c10", "b12", "c11", "b13", "c12", "c13",
    ),
)


def place(z_lo, y, z_hi, x, core):
    return (z_lo * 4 + y, z_hi * 8 + x * 2 + core)


def local_copy(src, dst, sem):
    copy = pltpu.make_async_copy(src, dst, sem)
    copy.start()


def send(src, dst, send_sem, recv_sem, device):
    copy = pltpu.make_async_remote_copy(
        src_ref=src,
        dst_ref=dst,
        send_sem=send_sem,
        recv_sem=recv_sem,
        device_id=device,
        device_id_type=MESH,
    )
    copy.start()


def wait_bytes(view, sem):
    pltpu.make_async_copy(view, view, sem).wait()


def dot(a, b):
    return jnp.dot(a, b, preferred_element_type=F32)


def kernel(
    stream, heads, w_out, gain_hbm, ids_hbm, gates_hbm, w_gate, w_up, w_down,
    out,
    heads_in, w_out_pair, proj_out, proj_in, stream_v, gate_w, up_w, down_w,
    gain, ids, gates, spread, pick, gate_col,
    payload, tokens, pre, pre_in, squares, squares_in, act,
    far_out, right_out, left_out, kept, far_left, far_right, from_left, from_right, summed, final_in,
    in_sem, w_sem, wr_sem, ws_sem,
    p1_recv, p1_send, px_recv, px_send, rs_recv, rs_send,
    d1_recv, d1_send, d2_recv, d2_send, d3_recv, d3_send, ex_recv, ex_send,
    f_recv, f_send, g_recv, g_send, z_recv, z_send,
):
    row = lax.axis_index("row")
    col = lax.axis_index("col")
    z_lo, y = lax.div(row, 4), lax.rem(row, 4)
    z_hi = lax.div(col, 8)
    x = lax.rem(lax.div(col, 2), 4)
    core = lax.rem(col, 2)
    other = 1 - core
    right = lax.rem(x + 1, 4)
    left = lax.rem(x + 3, 4)
    far = lax.rem(x + 2, 4)
    closers = []

    def finish():
        for close in closers:
            close()

    def later(view, sem):
        closers.append(lambda: wait_bytes(view, sem))

    def later_if(condition, view, sem):
        def close():
            @pl.when(condition)
            def _():
                wait_bytes(view, sem)

        closers.append(close)

    right_dev = place(z_lo, y, z_hi, right, core)
    left_dev = place(z_lo, y, z_hi, left, core)
    pair_dev = place(z_lo, y, z_hi, x, other)

    barrier = pltpu.get_barrier_semaphore()
    p_row_lo = lax.div(z_hi, 2)
    p_row_y = lax.rem(z_hi, 2) * 2 + lax.div(x, 2)
    p_self = jnp.logical_and(jnp.logical_and(p_row_lo == z_lo, p_row_y == y), z_lo == core)
    rs_self = z_lo == core

    def greet(device):
        pl.semaphore_signal(barrier, inc=1, device_id=device, device_id_type=MESH)

    def greet_other(device):
        @pl.when(jnp.logical_or(device[0] != row, device[1] != col))
        def _():
            greet(device)

    greet(right_dev)
    greet(left_dev)
    greet(pair_dev)
    for from_y in range(4):
        for from_x in range(2):
            for from_core in range(2):
                greet_other(
                    place(core, from_y, 2 * z_lo + lax.div(y, 2), 2 * lax.rem(y, 2) + from_x, from_core)
                )
    for from_lo in range(2):
        for from_y in range(4):
            greet_other(place(from_lo, from_y, z_hi, x, z_lo))
    pl.semaphore_wait(barrier, 27 - p_self.astype(jnp.int32) - rs_self.astype(jnp.int32))

    own_group = lax.rem(x, 2) * 2 + core
    for dz in (2, 1, 3, 0):
        for dx in (2, 1, 3, 0):
            to_x = lax.rem(x + dx, 4)
            to_z = lax.rem(z_hi + dz, 4)
            src = heads.at[pl.ds(to_x * 32, 32), :]
            dst = heads_in.at[to_x, own_group, y]
            device = place(p_row_lo, p_row_y, to_z, to_x, z_lo)
            if dz == 0 and dx == 0:
                @pl.when(p_self)
                def _():
                    local_copy(src, dst, p1_recv)

                @pl.when(jnp.logical_not(p_self))
                def _():
                    send(src, dst, p1_send.at[1], p1_recv, device)
            else:
                send(src, dst, p1_send.at[0], p1_recv, device)

    later(payload.at[0:15], p1_send.at[0])
    later_if(jnp.logical_not(p_self), payload.at[0], p1_send.at[1])

    local_copy(w_out, w_out_pair.at[core], w_sem.at[0])
    send(w_out, w_out_pair.at[core], ws_sem.at[0], wr_sem.at[0], pair_dev)
    local_copy(ids_hbm, ids, in_sem.at[1])
    local_copy(gates_hbm, gates, in_sem.at[2])
    local_copy(stream, stream_v, in_sem.at[0])
    local_copy(gain_hbm, gain, in_sem.at[3])
    local_copy(w_gate.at[:, core], gate_w.at[core], w_sem.at[1])
    local_copy(w_up.at[:, core], up_w.at[core], w_sem.at[2])
    send(w_gate.at[:, other], gate_w.at[core], ws_sem.at[1], wr_sem.at[1], pair_dev)
    send(w_up.at[:, other], up_w.at[core], ws_sem.at[2], wr_sem.at[2], pair_dev)

    def load_down(b, carry):
        mine = pl.multiple_of((2 * b + core) * 256, 256)
        theirs = pl.multiple_of((2 * b + other) * 256, 256)
        local_copy(w_down.at[:, pl.ds(mine, 256)], down_w.at[core, b], w_sem.at[3])
        send(w_down.at[:, pl.ds(theirs, 256)], down_w.at[core, b], ws_sem.at[3], wr_sem.at[3], pair_dev)
        return carry

    lax.fori_loop(0, 16, load_down, 0)
    later(w_out, ws_sem.at[0])
    later(gate_w.at[0], ws_sem.at[1])
    later(up_w.at[0], ws_sem.at[2])
    later(down_w.at[0], ws_sem.at[3])

    wait_bytes(ids, in_sem.at[1])
    wait_bytes(gates, in_sem.at[2])
    expert_sub = lax.broadcasted_iota(jnp.int32, (16, 128), 0)
    lane = lax.broadcasted_iota(jnp.int32, (128, 128), 1)
    sub = lax.broadcasted_iota(jnp.int32, (128, 128), 0)
    first = (ids[0:1, :] == expert_sub).astype(F32)
    second = (ids[1:2, :] == expert_sub).astype(F32)
    earlier = dot((first + second).astype(BF), (sub < lane).astype(BF))
    slot_sub = lax.broadcasted_iota(jnp.int32, (512, 128), 0)
    slot0 = ids[0:1, :] * 32 + jnp.sum(earlier * first, axis=0, keepdims=True).astype(jnp.int32)
    slot1 = ids[1:2, :] * 32 + jnp.sum(earlier * second, axis=0, keepdims=True).astype(jnp.int32)
    match0 = (slot0 == slot_sub).astype(F32)
    match1 = (slot1 == slot_sub).astype(F32)
    spread[...] = (match0 + match1).astype(BF)
    pick[0] = match0.T.astype(BF)
    pick[1] = match1.T.astype(BF)
    for k in range(2):
        gate_col[k] = jnp.broadcast_to(gates[k:k + 1, :], (128, 128)).T
    pre[...] = jnp.zeros_like(pre)
    squares[...] = jnp.zeros_like(squares)

    def project(group):
        rows = [heads_in[group, j].reshape(128, 256) for j in range(4)]
        for dc in range(2):
            c = core if dc == 0 else other
            total = dot(rows[0], w_out_pair[c, 0:256, :])
            for j in range(1, 4):
                total = total + dot(rows[j], w_out_pair[c, j * 256:(j + 1) * 256, :])
            proj_out[group, c] = total.astype(BF).reshape(4, 32, 256)
        for dy in (2, 1, 3, 0):
            to_y = lax.rem(y + dy, 4)
            for dc in range(2):
                c = core if dc == 0 else other
                src = proj_out.at[group, c, to_y]
                dst = proj_in.at[row, pl.ds(group * 32, 32), :]
                device = place(core, to_y, z_hi, x, c)
                if dy == 0 and dc == 0:
                    @pl.when(rs_self)
                    def _():
                        local_copy(src, dst, rs_recv)

                    @pl.when(jnp.logical_not(rs_self))
                    def _():
                        send(src, dst, rs_send.at[1], rs_recv, device)
                else:
                    send(src, dst, rs_send.at[0], rs_recv, device)

    wait_bytes(heads_in.at[x], p1_recv)
    later(final_in.at[0:7], rs_send.at[0])
    later_if(jnp.logical_not(rs_self), payload.at[0:4], rs_send.at[1])
    ends = (heads_in.at[x, 0:2], heads_in.at[x, 2:4])
    for k in range(2):
        send(ends[k], ends[k], px_send.at[0, k], px_recv.at[0, k], right_dev)
        send(ends[1 - k], ends[1 - k], px_send.at[1, k], px_recv.at[1, k], left_dev)
    wait_bytes(w_out_pair.at[core], w_sem.at[0])
    wait_bytes(w_out_pair.at[other], wr_sem.at[0])
    project(x)
    view = heads_in.at[left, 0:2]
    wait_bytes(view, px_recv.at[0, 0])
    send(view, view, px_send.at[0, 2], px_recv.at[0, 2], right_dev)
    view = heads_in.at[right, 2:4]
    wait_bytes(view, px_recv.at[1, 0])
    send(view, view, px_send.at[1, 2], px_recv.at[1, 2], left_dev)
    for way in range(2):
        for k in range(3):
            later(heads_in.at[0, 0:2], px_send.at[way, k])
    wait_bytes(heads_in.at[left, 2:4], px_recv.at[0, 1])
    project(left)
    wait_bytes(heads_in.at[right, 0:2], px_recv.at[1, 1])
    project(right)
    wait_bytes(heads_in.at[far, 0:2], px_recv.at[0, 2])
    wait_bytes(heads_in.at[far, 2:4], px_recv.at[1, 2])
    project(far)

    wait_bytes(stream_v, in_sem.at[0])
    wait_bytes(proj_in, rs_recv)
    residual = stream_v[...].astype(F32)
    for r in range(8):
        residual = residual + proj_in[r].astype(F32)
    stream_v[...] = residual.astype(BF)
    payload[...] = dot(spread[...], stream_v[...]).astype(BF).reshape(16, 32, 256)

    def dispatch(h, dz):
        to_z = lax.rem(z_hi + dz, 4)
        for step, dy in enumerate(Y_STEPS[h]):
            to_y = lax.rem(y + dy, 4)
            for dl in (1, 0):
                to_lo = z_lo if dl == 0 else 1 - z_lo
                expert = 2 * (to_lo * 4 + to_y) + lax.div(to_z, 2)
                src = payload.at[expert]
                dst = tokens.at[h, x, z_hi, step * 2 + z_lo]
                if dz == 0 and dl == 0 and dy == 0:
                    local_copy(src, dst, d1_recv.at[h, dz])
                else:
                    send(src, dst, d1_send.at[h, dz], d1_recv.at[h, dz], place(to_lo, to_y, to_z, x, core))
        later(payload.at[0:BLOCKS[h] - (dz == 0 and 0 in Y_STEPS[h])], d1_send.at[h, dz])

    def absorb(h, from_x, from_z):
        n = BLOCKS[h] * 32
        block = tokens[h, from_x, from_z, 0:BLOCKS[h]].reshape(n, 256).astype(F32)
        square = block * block
        squares[h, 0:n] += square[:, 0:128] + square[:, 128:256]
        scaled = (block * gain[from_z * 8 + from_x * 2 + core]).astype(BF)
        b = from_z * 4 + from_x
        for c in range(2):
            pre[h, c, 0:n] += dot(scaled, gate_w[c, b])
            pre[h, 2 + c, 0:n] += dot(scaled, up_w[c, b])

    def chunk_z(i):
        return lax.rem(z_hi + 4 - CHUNK_ORDER_IN[i], 4)

    def gather_first(h, i):
        zc = chunk_z(i)
        n = BLOCKS[h]
        wait_bytes(tokens.at[h, x, zc, 0:n], d1_recv.at[h, CHUNK_ORDER_IN[i]])
        ends = (tokens.at[h, x, zc, 0:n // 2], tokens.at[h, x, zc, n // 2:n])
        for k in range(2):
            send(ends[k], ends[k], d2_send.at[h, 0, i, k], d2_recv.at[h, 0, i, k], right_dev)
            send(ends[1 - k], ends[1 - k], d2_send.at[h, 1, i, k], d2_recv.at[h, 1, i, k], left_dev)
            for way in range(2):
                later(payload.at[0:n // 2], d2_send.at[h, way, i, k])
        absorb(h, x, zc)

    def gather_second(h, i):
        zc = chunk_z(i)
        n = BLOCKS[h]
        view = tokens.at[h, left, zc, 0:n // 2]
        wait_bytes(view, d2_recv.at[h, 0, i, 0])
        send(view, view, d3_send.at[h, 0, i], d3_recv.at[h, 0, i], right_dev)
        view = tokens.at[h, right, zc, n // 2:n]
        wait_bytes(view, d2_recv.at[h, 1, i, 0])
        send(view, view, d3_send.at[h, 1, i], d3_recv.at[h, 1, i], left_dev)
        for way in range(2):
            later(payload.at[0:n // 2], d3_send.at[h, way, i])
        wait_bytes(tokens.at[h, left, zc, n // 2:n], d2_recv.at[h, 0, i, 1])
        absorb(h, left, zc)
        wait_bytes(tokens.at[h, right, zc, 0:n // 2], d2_recv.at[h, 1, i, 1])
        absorb(h, right, zc)

    def gather_third(h, i):
        zc = chunk_z(i)
        n = BLOCKS[h]
        wait_bytes(tokens.at[h, far, zc, 0:n // 2], d3_recv.at[h, 0, i])
        wait_bytes(tokens.at[h, far, zc, n // 2:n], d3_recv.at[h, 1, i])
        absorb(h, far, zc)

    def exchange_first(h):
        n = BLOCKS[h] * 32
        sent, landed = pre.at[h, :, 0:n], pre_in.at[h, :, 0:n]
        send(sent, landed, ex_send.at[h, 0], ex_recv.at[h, 0], pair_dev)
        later(sent, ex_send.at[h, 0])
        sent, landed = squares.at[h, 0:n], squares_in.at[h, 0:n]
        send(sent, landed, ex_send.at[h, 1], ex_recv.at[h, 1], pair_dev)
        later(sent, ex_send.at[h, 1])

    def exchange_second(h):
        n = BLOCKS[h] * 32
        wait_bytes(squares_in.at[h, 0:n], ex_recv.at[h, 1])
        wait_bytes(pre_in.at[h, :, 0:n], ex_recv.at[h, 0])
        mean = jnp.sum(squares[h, 0:n] + squares_in[h, 0:n], axis=1, keepdims=True) / WIDTH
        scale = lax.rsqrt(mean + 1e-05)
        for c in range(2):
            gate_pre = (pre[h, c, 0:n] + pre_in[h, c, 0:n]) * scale
            up_pre = (pre[h, 2 + c, 0:n] + pre_in[h, 2 + c, 0:n]) * scale
            act[h, c, 0:n] = (gate_pre / (1.0 + jnp.exp(-gate_pre)) * up_pre).astype(BF)

    def down(h, to_x, zc):
        b = zc * 4 + to_x
        n = BLOCKS[h] * 32
        return dot(act[h, 0, 0:n], down_w[0, b]) + dot(act[h, 1, 0:n], down_w[1, b])

    def out_z(i):
        return lax.rem(z_hi + CHUNK_ORDER_OUT[i], 4)

    def return_first(h, i):
        zc = out_z(i)
        n = BLOCKS[h] * 32
        m = n // 2
        far_out[h, i, 0:n] = down(h, far, zc).astype(BF)
        send(far_out.at[h, i, 0:m], far_left.at[h, i, 0:m], f_send.at[h, 0, i], f_recv.at[h, 0, i], right_dev)
        send(far_out.at[h, i, m:n], far_right.at[h, i, 0:m], f_send.at[h, 1, i], f_recv.at[h, 1, i], left_dev)
        mine = down(h, right, zc)
        right_out[h, i, m:n] = mine[m:n].astype(BF)
        send(right_out.at[h, i, m:n], from_left.at[h, i, m:n], g_send.at[h, 0, i], g_recv.at[h, 0, i], right_dev)
        kept[h, i, 0, 0:m] = mine[0:m]
        mine = down(h, left, zc)
        left_out[h, i, 0:m] = mine[0:m].astype(BF)
        send(left_out.at[h, i, 0:m], from_right.at[h, i, 0:m], g_send.at[h, 1, i], g_recv.at[h, 1, i], left_dev)
        kept[h, i, 1, 0:m] = mine[m:n]
        for way in range(2):
            later(far_left.at[h, i, 0:m], f_send.at[h, way, i])

    def return_second(h, i):
        n = BLOCKS[h] * 32
        m = n // 2
        wait_bytes(far_left.at[h, i, 0:m], f_recv.at[h, 0, i])
        right_out[h, i, 0:m] = (kept[h, i, 0, 0:m] + far_left[h, i, 0:m].astype(F32)).astype(BF)
        send(right_out.at[h, i, 0:m], from_left.at[h, i, 0:m], g_send.at[h, 0, i], g_recv.at[h, 0, i], right_dev)
        wait_bytes(far_right.at[h, i, 0:m], f_recv.at[h, 1, i])
        left_out[h, i, m:n] = (kept[h, i, 1, 0:m] + far_right[h, i, 0:m].astype(F32)).astype(BF)
        send(left_out.at[h, i, m:n], from_right.at[h, i, m:n], g_send.at[h, 1, i], g_recv.at[h, 1, i], left_dev)
        for way in range(2):
            later(from_left.at[h, i, 0:n], g_send.at[h, way, i])

    def return_third(h, i):
        zc = out_z(i)
        n = BLOCKS[h] * 32
        mine = down(h, x, zc)
        wait_bytes(from_left.at[h, i, 0:n], g_recv.at[h, 0, i])
        wait_bytes(from_right.at[h, i, 0:n], g_recv.at[h, 1, i])
        total = mine + from_left[h, i, 0:n].astype(F32) + from_right[h, i, 0:n].astype(F32)
        summed[h, i, 0:BLOCKS[h]] = total.astype(BF).reshape(BLOCKS[h], 32, 256)
        near = CHUNK_ORDER_OUT[i] == 0
        for step, dy in enumerate(Y_STEPS[h]):
            to_y = lax.rem(y + 4 - dy, 4)
            for dl in (1, 0):
                to_lo = z_lo if dl == 0 else 1 - z_lo
                src = summed.at[h, i, step * 2 + to_lo]
                dst = final_in.at[row, z_hi]
                if near and dl == 0 and dy == 0:
                    local_copy(src, dst, z_recv)
                else:
                    send(src, dst, z_send.at[h, i], z_recv, place(to_lo, to_y, zc, x, core))
        later(payload.at[0:BLOCKS[h] - (near and 0 in Y_STEPS[h])], z_send.at[h, i])

    def wait_gate_up():
        wait_bytes(gain, in_sem.at[3])
        wait_bytes(gate_w.at[core], w_sem.at[1])
        wait_bytes(up_w.at[core], w_sem.at[2])
        wait_bytes(gate_w.at[other], wr_sem.at[1])
        wait_bytes(up_w.at[other], wr_sem.at[2])

    def wait_down():
        wait_bytes(down_w.at[core], w_sem.at[3])
        wait_bytes(down_w.at[other], wr_sem.at[3])

    steps = dict(
        d=dispatch, p=gather_first, q=gather_second, r=gather_third, e=exchange_first, f=exchange_second,
        a=return_first, b=return_second, c=return_third,
    )
    for part in PLAN:
        for name in part:
            step, h = steps[name[0]], int(name[1])
            if name[0] in "ef":
                step(h)
            else:
                step(h, int(name[2]))
        if part is PLAN[0]:
            wait_gate_up()
        if part is PLAN[1]:
            wait_down()

    wait_bytes(final_in, z_recv)
    pieces = final_in[...].astype(F32).reshape(16, 2, 32, 256)
    expert_out = (pieces[:, 0] + pieces[:, 1]).astype(BF).reshape(512, 256)
    picked0 = dot(pick[0], expert_out)
    picked1 = dot(pick[1], expert_out)
    mixed = stream_v[...].astype(F32) + (
        gate_col[0, :, 0:1] * picked0 + gate_col[1, :, 0:1] * picked1
    )
    out[...] = mixed.astype(BF)
    finish()


def per_device(stream, heads_out, w_out, norm_gain, expert_ids, route_gates, w_gate, w_up, w_down):
    hbm = pl.BlockSpec(memory_space=pl.ANY)
    vmem = pl.BlockSpec(memory_space=pltpu.VMEM)
    dma = pltpu.SemaphoreType.DMA
    scratch = [
        pltpu.VMEM((4, 4, 4, 32, 256), BF),
        pltpu.VMEM((2, 1024, 256), BF),
        pltpu.VMEM((4, 2, 4, 32, 256), BF),
        pltpu.VMEM((8, 128, 256), BF),
        pltpu.VMEM((128, 256), BF),
        pltpu.VMEM((2, 16, 256, 256), BF),
        pltpu.VMEM((2, 16, 256, 256), BF),
        pltpu.VMEM((2, 16, 256, 256), BF),
        pltpu.VMEM((32, 1, 256), F32),
        pltpu.VMEM((2, 128), jnp.int32),
        pltpu.VMEM((2, 128), F32),
        pltpu.VMEM((512, 128), BF),
        pltpu.VMEM((2, 128, 512), BF),
        pltpu.VMEM((2, 128, 128), F32),
        pltpu.VMEM((16, 32, 256), BF),
        pltpu.VMEM((PARTS, 4, 4, MOST, 32, 256), BF),
        pltpu.VMEM((PARTS, 4, MOST * 32, 256), F32),
        pltpu.VMEM((PARTS, 4, MOST * 32, 256), F32),
        pltpu.VMEM((PARTS, MOST * 32, 128), F32),
        pltpu.VMEM((PARTS, MOST * 32, 128), F32),
        pltpu.VMEM((PARTS, 2, MOST * 32, 256), BF),
        pltpu.VMEM((PARTS, 4, MOST * 32, 256), BF),
        pltpu.VMEM((PARTS, 4, MOST * 32, 256), BF),
        pltpu.VMEM((PARTS, 4, MOST * 32, 256), BF),
        pltpu.VMEM((PARTS, 4, 2, MOST * 16, 256), F32),
        pltpu.VMEM((PARTS, 4, MOST * 16, 256), BF),
        pltpu.VMEM((PARTS, 4, MOST * 16, 256), BF),
        pltpu.VMEM((PARTS, 4, MOST * 32, 256), BF),
        pltpu.VMEM((PARTS, 4, MOST * 32, 256), BF),
        pltpu.VMEM((PARTS, 4, MOST, 32, 256), BF),
        pltpu.VMEM((8, 4, 32, 256), BF),
        dma((4,)),
        dma((4,)),
        dma((4,)),
        dma((4,)),
        dma,
        dma((2,)),
        dma((2, 3)),
        dma((2, 3)),
        dma,
        dma((2,)),
        dma((PARTS, 4)),
        dma((PARTS, 4)),
        dma((PARTS, 2, 4, 2)),
        dma((PARTS, 2, 4, 2)),
        dma((PARTS, 2, 4)),
        dma((PARTS, 2, 4)),
        dma((PARTS, 2)),
        dma((PARTS, 2)),
        dma((PARTS, 2, 4)),
        dma((PARTS, 2, 4)),
        dma((PARTS, 2, 4)),
        dma((PARTS, 2, 4)),
        dma,
        dma((PARTS, 4)),
    ]
    return pl.pallas_call(
        kernel,
        out_shape=jax.ShapeDtypeStruct((128, 256), BF),
        in_specs=[hbm] * 9,
        out_specs=vmem,
        scratch_shapes=scratch,
        compiler_params=pltpu.CompilerParams(
            collective_id=0, has_side_effects=True, vmem_limit_bytes=60 * 1024 * 1024
        ),
        name="block",
    )(
        stream,
        heads_out,
        w_out,
        norm_gain.reshape(32, 1, 256),
        expert_ids.T,
        route_gates.T,
        w_gate.reshape(16, 2, 256, 256),
        w_up.reshape(16, 2, 256, 256),
        w_down,
    )


def solution(mesh):
    return jax.shard_map(
        per_device,
        mesh=mesh,
        in_specs=(
            P("row", "col"),
            P("row", "col"),
            P("row", "col"),
            P(),
            P("row", None),
            P("row", None),
            P(None, ("row", "col")),
            P(None, ("row", "col")),
            P(("row", "col"), None),
        ),
        out_specs=P("row", "col"),
        check_vma=False,
    )
```

```python
import jax
import jax.numpy as jnp
from jax import lax
from jax.experimental import pallas as pl
from jax.experimental.pallas import tpu as pltpu
from jax.sharding import PartitionSpec as P

MESH = pl.DeviceIdType.MESH
BF = jnp.bfloat16
F32 = jnp.float32
WIDTH = 8192
CHUNK_ORDER_IN = (0, 1, 3, 2)
CHUNK_ORDER_OUT = (2, 1, 3, 0)
Y_STEPS = ((0, 2), (1, 3))
PARTS = len(Y_STEPS)
BLOCKS = tuple(2 * len(part) for part in Y_STEPS)
MOST = max(BLOCKS)
PLAN = (
    (
        "d00", "d01", "d03", "d02",
    ),
    (
        "p00", "p01", "p02", "d10", "p03", "d11", "d13", "d12", "q00", "q01", "q02", "q03",
        "r00", "r01", "r02", "r03", "e0", "p10", "p11", "p12", "p13", "q10", "q11", "q12",
        "q13", "f0",
    ),
    (
        "a00", "a01", "a02", "a03", "r10", "r11", "r12", "r13", "e1", "b00", "b01", "b02",
        "b03", "f1", "a10", "a11", "c00", "c01", "b10", "a12", "b11", "a13", "c02", "c03",
        "c10", "b12", "c11", "b13", "c12", "c13",
    ),
)


def place(z_lo, y, z_hi, x, core):
    return (z_lo * 4 + y, z_hi * 8 + x * 2 + core)


def local_copy(src, dst, sem):
    copy = pltpu.make_async_copy(src, dst, sem)
    copy.start()


def send(src, dst, send_sem, recv_sem, device):
    copy = pltpu.make_async_remote_copy(
        src_ref=src,
        dst_ref=dst,
        send_sem=send_sem,
        recv_sem=recv_sem,
        device_id=device,
        device_id_type=MESH,
    )
    copy.start()


def wait_bytes(view, sem):
    pltpu.make_async_copy(view, view, sem).wait()


def dot(a, b):
    return jnp.dot(a, b, preferred_element_type=F32)


def kernel(
    stream, heads, w_out, gain_hbm, ids_hbm, gates_hbm, w_gate, w_up, w_down,
    out,
    heads_in, w_out_pair, proj_out, proj_in, stream_v, gate_w, up_w, down_w,
    gain, ids, gates, spread, pick, gate_col,
    payload, tokens, pre, pre_in, squares, squares_in, act,
    far_out, right_out, left_out, kept, far_left, far_right, from_left, from_right, summed, final_in,
    in_sem, w_sem, wr_sem, ws_sem,
    p1_recv, p1_send, px_recv, px_send, rs_recv, rs_send,
    d1_recv, d1_send, d2_recv, d2_send, d3_recv, d3_send, ex_recv, ex_send,
    f_recv, f_send, g_recv, g_send, z_recv, z_send,
):
    row = lax.axis_index("row")
    col = lax.axis_index("col")
    z_lo, y = lax.div(row, 4), lax.rem(row, 4)
    z_hi = lax.div(col, 8)
    x = lax.rem(lax.div(col, 2), 4)
    core = lax.rem(col, 2)
    other = 1 - core
    right = lax.rem(x + 1, 4)
    left = lax.rem(x + 3, 4)
    far = lax.rem(x + 2, 4)
    closers = []

    def finish():
        for close in closers:
            close()

    def later(view, sem):
        closers.append(lambda: wait_bytes(view, sem))

    def later_if(condition, view, sem):
        def close():
            @pl.when(condition)
            def _():
                wait_bytes(view, sem)

        closers.append(close)

    right_dev = place(z_lo, y, z_hi, right, core)
    left_dev = place(z_lo, y, z_hi, left, core)
    pair_dev = place(z_lo, y, z_hi, x, other)

    barrier = pltpu.get_barrier_semaphore()
    p_row_lo = lax.div(z_hi, 2)
    p_row_y = lax.rem(z_hi, 2) * 2 + lax.div(x, 2)
    p_self = jnp.logical_and(jnp.logical_and(p_row_lo == z_lo, p_row_y == y), z_lo == core)
    rs_self = z_lo == core

    def greet(device):
        pl.semaphore_signal(barrier, inc=1, device_id=device, device_id_type=MESH)

    def greet_other(device):
        @pl.when(jnp.logical_or(device[0] != row, device[1] != col))
        def _():
            greet(device)

    greet(right_dev)
    greet(left_dev)
    greet(pair_dev)
    for from_y in range(4):
        for from_x in range(2):
            for from_core in range(2):
                greet_other(
                    place(core, from_y, 2 * z_lo + lax.div(y, 2), 2 * lax.rem(y, 2) + from_x, from_core)
                )
    for from_lo in range(2):
        for from_y in range(4):
            greet_other(place(from_lo, from_y, z_hi, x, z_lo))
    pl.semaphore_wait(barrier, 27 - p_self.astype(jnp.int32) - rs_self.astype(jnp.int32))

    own_group = lax.rem(x, 2) * 2 + core
    for dz in (2, 1, 3, 0):
        for dx in (2, 1, 3, 0):
            to_x = lax.rem(x + dx, 4)
            to_z = lax.rem(z_hi + dz, 4)
            src = heads.at[pl.ds(to_x * 32, 32), :]
            dst = heads_in.at[to_x, own_group, y]
            device = place(p_row_lo, p_row_y, to_z, to_x, z_lo)
            if dz == 0 and dx == 0:
                @pl.when(p_self)
                def _():
                    local_copy(src, dst, p1_recv)

                @pl.when(jnp.logical_not(p_self))
                def _():
                    send(src, dst, p1_send.at[1], p1_recv, device)
            else:
                send(src, dst, p1_send.at[0], p1_recv, device)

    later(payload.at[0:15], p1_send.at[0])
    later_if(jnp.logical_not(p_self), payload.at[0], p1_send.at[1])

    local_copy(w_out, w_out_pair.at[core], w_sem.at[0])
    send(w_out, w_out_pair.at[core], ws_sem.at[0], wr_sem.at[0], pair_dev)
    local_copy(ids_hbm, ids, in_sem.at[1])
    local_copy(gates_hbm, gates, in_sem.at[2])
    local_copy(stream, stream_v, in_sem.at[0])
    local_copy(gain_hbm, gain, in_sem.at[3])
    local_copy(w_gate.at[:, core], gate_w.at[core], w_sem.at[1])
    local_copy(w_up.at[:, core], up_w.at[core], w_sem.at[2])
    send(w_gate.at[:, other], gate_w.at[core], ws_sem.at[1], wr_sem.at[1], pair_dev)
    send(w_up.at[:, other], up_w.at[core], ws_sem.at[2], wr_sem.at[2], pair_dev)

    def load_down(b, carry):
        mine = pl.multiple_of((2 * b + core) * 256, 256)
        theirs = pl.multiple_of((2 * b + other) * 256, 256)
        local_copy(w_down.at[:, pl.ds(mine, 256)], down_w.at[core, b], w_sem.at[3])
        send(w_down.at[:, pl.ds(theirs, 256)], down_w.at[core, b], ws_sem.at[3], wr_sem.at[3], pair_dev)
        return carry

    lax.fori_loop(0, 16, load_down, 0)
    later(w_out, ws_sem.at[0])
    later(gate_w.at[0], ws_sem.at[1])
    later(up_w.at[0], ws_sem.at[2])
    later(down_w.at[0], ws_sem.at[3])

    wait_bytes(ids, in_sem.at[1])
    wait_bytes(gates, in_sem.at[2])
    expert_sub = lax.broadcasted_iota(jnp.int32, (16, 128), 0)
    lane = lax.broadcasted_iota(jnp.int32, (128, 128), 1)
    sub = lax.broadcasted_iota(jnp.int32, (128, 128), 0)
    first = (ids[0:1, :] == expert_sub).astype(F32)
    second = (ids[1:2, :] == expert_sub).astype(F32)
    earlier = dot((first + second).astype(BF), (sub < lane).astype(BF))
    slot_sub = lax.broadcasted_iota(jnp.int32, (512, 128), 0)
    slot0 = ids[0:1, :] * 32 + jnp.sum(earlier * first, axis=0, keepdims=True).astype(jnp.int32)
    slot1 = ids[1:2, :] * 32 + jnp.sum(earlier * second, axis=0, keepdims=True).astype(jnp.int32)
    match0 = (slot0 == slot_sub).astype(F32)
    match1 = (slot1 == slot_sub).astype(F32)
    spread[...] = (match0 + match1).astype(BF)
    pick[0] = match0.T.astype(BF)
    pick[1] = match1.T.astype(BF)
    for k in range(2):
        gate_col[k] = jnp.broadcast_to(gates[k:k + 1, :], (128, 128)).T
    pre[...] = jnp.zeros_like(pre)
    squares[...] = jnp.zeros_like(squares)

    def project(group):
        rows = [heads_in[group, j].reshape(128, 256) for j in range(4)]
        for dc in range(2):
            c = core if dc == 0 else other
            total = dot(rows[0], w_out_pair[c, 0:256, :])
            for j in range(1, 4):
                total = total + dot(rows[j], w_out_pair[c, j * 256:(j + 1) * 256, :])
            proj_out[group, c] = total.astype(BF).reshape(4, 32, 256)
        for dy in (2, 1, 3, 0):
            to_y = lax.rem(y + dy, 4)
            for dc in range(2):
                c = core if dc == 0 else other
                src = proj_out.at[group, c, to_y]
                dst = proj_in.at[row, pl.ds(group * 32, 32), :]
                device = place(core, to_y, z_hi, x, c)
                if dy == 0 and dc == 0:
                    @pl.when(rs_self)
                    def _():
                        local_copy(src, dst, rs_recv)

                    @pl.when(jnp.logical_not(rs_self))
                    def _():
                        send(src, dst, rs_send.at[1], rs_recv, device)
                else:
                    send(src, dst, rs_send.at[0], rs_recv, device)

    wait_bytes(heads_in.at[x], p1_recv)
    later(final_in.at[0:7], rs_send.at[0])
    later_if(jnp.logical_not(rs_self), payload.at[0:4], rs_send.at[1])
    ends = (heads_in.at[x, 0:2], heads_in.at[x, 2:4])
    for k in range(2):
        send(ends[k], ends[k], px_send.at[0, k], px_recv.at[0, k], right_dev)
        send(ends[1 - k], ends[1 - k], px_send.at[1, k], px_recv.at[1, k], left_dev)
    wait_bytes(w_out_pair.at[core], w_sem.at[0])
    wait_bytes(w_out_pair.at[other], wr_sem.at[0])
    project(x)
    view = heads_in.at[left, 0:2]
    wait_bytes(view, px_recv.at[0, 0])
    send(view, view, px_send.at[0, 2], px_recv.at[0, 2], right_dev)
    view = heads_in.at[right, 2:4]
    wait_bytes(view, px_recv.at[1, 0])
    send(view, view, px_send.at[1, 2], px_recv.at[1, 2], left_dev)
    for way in range(2):
        for k in range(3):
            later(heads_in.at[0, 0:2], px_send.at[way, k])
    wait_bytes(heads_in.at[left, 2:4], px_recv.at[0, 1])
    project(left)
    wait_bytes(heads_in.at[right, 0:2], px_recv.at[1, 1])
    project(right)
    wait_bytes(heads_in.at[far, 0:2], px_recv.at[0, 2])
    wait_bytes(heads_in.at[far, 2:4], px_recv.at[1, 2])
    project(far)

    wait_bytes(stream_v, in_sem.at[0])
    wait_bytes(proj_in, rs_recv)
    residual = stream_v[...].astype(F32)
    for r in range(8):
        residual = residual + proj_in[r].astype(F32)
    stream_v[...] = residual.astype(BF)
    payload[...] = dot(spread[...], stream_v[...]).astype(BF).reshape(16, 32, 256)

    def dispatch(h, dz):
        to_z = lax.rem(z_hi + dz, 4)
        for step, dy in enumerate(Y_STEPS[h]):
            to_y = lax.rem(y + dy, 4)
            for dl in (1, 0):
                to_lo = z_lo if dl == 0 else 1 - z_lo
                expert = 2 * (to_lo * 4 + to_y) + lax.div(to_z, 2)
                src = payload.at[expert]
                dst = tokens.at[h, x, z_hi, step * 2 + z_lo]
                if dz == 0 and dl == 0 and dy == 0:
                    local_copy(src, dst, d1_recv.at[h, dz])
                else:
                    send(src, dst, d1_send.at[h, dz], d1_recv.at[h, dz], place(to_lo, to_y, to_z, x, core))
        later(payload.at[0:BLOCKS[h] - (dz == 0 and 0 in Y_STEPS[h])], d1_send.at[h, dz])

    def absorb(h, from_x, from_z):
        n = BLOCKS[h] * 32
        block = tokens[h, from_x, from_z, 0:BLOCKS[h]].reshape(n, 256).astype(F32)
        square = block * block
        squares[h, 0:n] += square[:, 0:128] + square[:, 128:256]
        scaled = (block * gain[from_z * 8 + from_x * 2 + core]).astype(BF)
        b = from_z * 4 + from_x
        for c in range(2):
            pre[h, c, 0:n] += dot(scaled, gate_w[c, b])
            pre[h, 2 + c, 0:n] += dot(scaled, up_w[c, b])

    def chunk_z(i):
        return lax.rem(z_hi + 4 - CHUNK_ORDER_IN[i], 4)

    def gather_first(h, i):
        zc = chunk_z(i)
        n = BLOCKS[h]
        wait_bytes(tokens.at[h, x, zc, 0:n], d1_recv.at[h, CHUNK_ORDER_IN[i]])
        view = tokens.at[h, x, zc, 0:n]
        send(view, view, d2_send.at[h, 0, i], d2_recv.at[h, 0, i], right_dev)
        send(view, view, d2_send.at[h, 1, i], d2_recv.at[h, 1, i], left_dev)
        for way in range(2):
            later(payload.at[0:n], d2_send.at[h, way, i])
        absorb(h, x, zc)

    def gather_second(h, i):
        zc = chunk_z(i)
        n = BLOCKS[h]
        wait_bytes(tokens.at[h, left, zc, 0:n], d2_recv.at[h, 0, i])
        view = tokens.at[h, left, zc, 0:n // 2]
        send(view, view, d3_send.at[h, 0, i], d3_recv.at[h, 0, i], right_dev)
        wait_bytes(tokens.at[h, right, zc, 0:n], d2_recv.at[h, 1, i])
        view = tokens.at[h, right, zc, n // 2:n]
        send(view, view, d3_send.at[h, 1, i], d3_recv.at[h, 1, i], left_dev)
        for way in range(2):
            later(payload.at[0:n // 2], d3_send.at[h, way, i])
        absorb(h, left, zc)
        absorb(h, right, zc)

    def gather_third(h, i):
        zc = chunk_z(i)
        n = BLOCKS[h]
        wait_bytes(tokens.at[h, far, zc, 0:n // 2], d3_recv.at[h, 0, i])
        wait_bytes(tokens.at[h, far, zc, n // 2:n], d3_recv.at[h, 1, i])
        absorb(h, far, zc)

    def exchange_first(h):
        n = BLOCKS[h] * 32
        sent, landed = pre.at[h, :, 0:n], pre_in.at[h, :, 0:n]
        send(sent, landed, ex_send.at[h, 0], ex_recv.at[h, 0], pair_dev)
        later(sent, ex_send.at[h, 0])
        sent, landed = squares.at[h, 0:n], squares_in.at[h, 0:n]
        send(sent, landed, ex_send.at[h, 1], ex_recv.at[h, 1], pair_dev)
        later(sent, ex_send.at[h, 1])

    def exchange_second(h):
        n = BLOCKS[h] * 32
        wait_bytes(squares_in.at[h, 0:n], ex_recv.at[h, 1])
        wait_bytes(pre_in.at[h, :, 0:n], ex_recv.at[h, 0])
        mean = jnp.sum(squares[h, 0:n] + squares_in[h, 0:n], axis=1, keepdims=True) / WIDTH
        scale = lax.rsqrt(mean + 1e-05)
        for c in range(2):
            gate_pre = (pre[h, c, 0:n] + pre_in[h, c, 0:n]) * scale
            up_pre = (pre[h, 2 + c, 0:n] + pre_in[h, 2 + c, 0:n]) * scale
            act[h, c, 0:n] = (gate_pre / (1.0 + jnp.exp(-gate_pre)) * up_pre).astype(BF)

    def down(h, to_x, zc):
        b = zc * 4 + to_x
        n = BLOCKS[h] * 32
        return dot(act[h, 0, 0:n], down_w[0, b]) + dot(act[h, 1, 0:n], down_w[1, b])

    def out_z(i):
        return lax.rem(z_hi + CHUNK_ORDER_OUT[i], 4)

    def return_first(h, i):
        zc = out_z(i)
        n = BLOCKS[h] * 32
        m = n // 2
        far_out[h, i, 0:n] = down(h, far, zc).astype(BF)
        send(far_out.at[h, i, 0:m], far_left.at[h, i, 0:m], f_send.at[h, 0, i], f_recv.at[h, 0, i], right_dev)
        send(far_out.at[h, i, m:n], far_right.at[h, i, 0:m], f_send.at[h, 1, i], f_recv.at[h, 1, i], left_dev)
        mine = down(h, right, zc)
        right_out[h, i, m:n] = mine[m:n].astype(BF)
        send(right_out.at[h, i, m:n], from_left.at[h, i, m:n], g_send.at[h, 0, i], g_recv.at[h, 0, i], right_dev)
        kept[h, i, 0, 0:m] = mine[0:m]
        mine = down(h, left, zc)
        left_out[h, i, 0:m] = mine[0:m].astype(BF)
        send(left_out.at[h, i, 0:m], from_right.at[h, i, 0:m], g_send.at[h, 1, i], g_recv.at[h, 1, i], left_dev)
        kept[h, i, 1, 0:m] = mine[m:n]
        for way in range(2):
            later(far_left.at[h, i, 0:m], f_send.at[h, way, i])

    def return_second(h, i):
        n = BLOCKS[h] * 32
        m = n // 2
        wait_bytes(far_left.at[h, i, 0:m], f_recv.at[h, 0, i])
        right_out[h, i, 0:m] = (kept[h, i, 0, 0:m] + far_left[h, i, 0:m].astype(F32)).astype(BF)
        send(right_out.at[h, i, 0:m], from_left.at[h, i, 0:m], g_send.at[h, 0, i], g_recv.at[h, 0, i], right_dev)
        wait_bytes(far_right.at[h, i, 0:m], f_recv.at[h, 1, i])
        left_out[h, i, m:n] = (kept[h, i, 1, 0:m] + far_right[h, i, 0:m].astype(F32)).astype(BF)
        send(left_out.at[h, i, m:n], from_right.at[h, i, m:n], g_send.at[h, 1, i], g_recv.at[h, 1, i], left_dev)
        for way in range(2):
            later(from_left.at[h, i, 0:n], g_send.at[h, way, i])

    def return_third(h, i):
        zc = out_z(i)
        n = BLOCKS[h] * 32
        mine = down(h, x, zc)
        wait_bytes(from_left.at[h, i, 0:n], g_recv.at[h, 0, i])
        wait_bytes(from_right.at[h, i, 0:n], g_recv.at[h, 1, i])
        total = mine + from_left[h, i, 0:n].astype(F32) + from_right[h, i, 0:n].astype(F32)
        summed[h, i, 0:BLOCKS[h]] = total.astype(BF).reshape(BLOCKS[h], 32, 256)
        near = CHUNK_ORDER_OUT[i] == 0
        for step, dy in enumerate(Y_STEPS[h]):
            to_y = lax.rem(y + 4 - dy, 4)
            for dl in (1, 0):
                to_lo = z_lo if dl == 0 else 1 - z_lo
                src = summed.at[h, i, step * 2 + to_lo]
                dst = final_in.at[row, z_hi]
                if near and dl == 0 and dy == 0:
                    local_copy(src, dst, z_recv)
                else:
                    send(src, dst, z_send.at[h, i], z_recv, place(to_lo, to_y, zc, x, core))
        later(payload.at[0:BLOCKS[h] - (near and 0 in Y_STEPS[h])], z_send.at[h, i])

    def wait_gate_up():
        wait_bytes(gain, in_sem.at[3])
        wait_bytes(gate_w.at[core], w_sem.at[1])
        wait_bytes(up_w.at[core], w_sem.at[2])
        wait_bytes(gate_w.at[other], wr_sem.at[1])
        wait_bytes(up_w.at[other], wr_sem.at[2])

    def wait_down():
        wait_bytes(down_w.at[core], w_sem.at[3])
        wait_bytes(down_w.at[other], wr_sem.at[3])

    steps = dict(
        d=dispatch, p=gather_first, q=gather_second, r=gather_third, e=exchange_first, f=exchange_second,
        a=return_first, b=return_second, c=return_third,
    )
    for part in PLAN:
        for name in part:
            step, h = steps[name[0]], int(name[1])
            if name[0] in "ef":
                step(h)
            else:
                step(h, int(name[2]))
        if part is PLAN[0]:
            wait_gate_up()
        if part is PLAN[1]:
            wait_down()

    wait_bytes(final_in, z_recv)
    pieces = final_in[...].astype(F32).reshape(16, 2, 32, 256)
    expert_out = (pieces[:, 0] + pieces[:, 1]).astype(BF).reshape(512, 256)
    picked0 = dot(pick[0], expert_out)
    picked1 = dot(pick[1], expert_out)
    mixed = stream_v[...].astype(F32) + (
        gate_col[0, :, 0:1] * picked0 + gate_col[1, :, 0:1] * picked1
    )
    out[...] = mixed.astype(BF)
    finish()


def per_device(stream, heads_out, w_out, norm_gain, expert_ids, route_gates, w_gate, w_up, w_down):
    hbm = pl.BlockSpec(memory_space=pl.ANY)
    vmem = pl.BlockSpec(memory_space=pltpu.VMEM)
    dma = pltpu.SemaphoreType.DMA
    scratch = [
        pltpu.VMEM((4, 4, 4, 32, 256), BF),
        pltpu.VMEM((2, 1024, 256), BF),
        pltpu.VMEM((4, 2, 4, 32, 256), BF),
        pltpu.VMEM((8, 128, 256), BF),
        pltpu.VMEM((128, 256), BF),
        pltpu.VMEM((2, 16, 256, 256), BF),
        pltpu.VMEM((2, 16, 256, 256), BF),
        pltpu.VMEM((2, 16, 256, 256), BF),
        pltpu.VMEM((32, 1, 256), F32),
        pltpu.VMEM((2, 128), jnp.int32),
        pltpu.VMEM((2, 128), F32),
        pltpu.VMEM((512, 128), BF),
        pltpu.VMEM((2, 128, 512), BF),
        pltpu.VMEM((2, 128, 128), F32),
        pltpu.VMEM((16, 32, 256), BF),
        pltpu.VMEM((PARTS, 4, 4, MOST, 32, 256), BF),
        pltpu.VMEM((PARTS, 4, MOST * 32, 256), F32),
        pltpu.VMEM((PARTS, 4, MOST * 32, 256), F32),
        pltpu.VMEM((PARTS, MOST * 32, 128), F32),
        pltpu.VMEM((PARTS, MOST * 32, 128), F32),
        pltpu.VMEM((PARTS, 2, MOST * 32, 256), BF),
        pltpu.VMEM((PARTS, 4, MOST * 32, 256), BF),
        pltpu.VMEM((PARTS, 4, MOST * 32, 256), BF),
        pltpu.VMEM((PARTS, 4, MOST * 32, 256), BF),
        pltpu.VMEM((PARTS, 4, 2, MOST * 16, 256), F32),
        pltpu.VMEM((PARTS, 4, MOST * 16, 256), BF),
        pltpu.VMEM((PARTS, 4, MOST * 16, 256), BF),
        pltpu.VMEM((PARTS, 4, MOST * 32, 256), BF),
        pltpu.VMEM((PARTS, 4, MOST * 32, 256), BF),
        pltpu.VMEM((PARTS, 4, MOST, 32, 256), BF),
        pltpu.VMEM((8, 4, 32, 256), BF),
        dma((4,)),
        dma((4,)),
        dma((4,)),
        dma((4,)),
        dma,
        dma((2,)),
        dma((2, 3)),
        dma((2, 3)),
        dma,
        dma((2,)),
        dma((PARTS, 4)),
        dma((PARTS, 4)),
        dma((PARTS, 2, 4)),
        dma((PARTS, 2, 4)),
        dma((PARTS, 2, 4)),
        dma((PARTS, 2, 4)),
        dma((PARTS, 2)),
        dma((PARTS, 2)),
        dma((PARTS, 2, 4)),
        dma((PARTS, 2, 4)),
        dma((PARTS, 2, 4)),
        dma((PARTS, 2, 4)),
        dma,
        dma((PARTS, 4)),
    ]
    return pl.pallas_call(
        kernel,
        out_shape=jax.ShapeDtypeStruct((128, 256), BF),
        in_specs=[hbm] * 9,
        out_specs=vmem,
        scratch_shapes=scratch,
        compiler_params=pltpu.CompilerParams(
            collective_id=0, has_side_effects=True, vmem_limit_bytes=60 * 1024 * 1024
        ),
        name="block",
    )(
        stream,
        heads_out,
        w_out,
        norm_gain.reshape(32, 1, 256),
        expert_ids.T,
        route_gates.T,
        w_gate.reshape(16, 2, 256, 256),
        w_up.reshape(16, 2, 256, 256),
        w_down,
    )


def solution(mesh):
    return jax.shard_map(
        per_device,
        mesh=mesh,
        in_specs=(
            P("row", "col"),
            P("row", "col"),
            P("row", "col"),
            P(),
            P("row", None),
            P("row", None),
            P(None, ("row", "col")),
            P(None, ("row", "col")),
            P(("row", "col"), None),
        ),
        out_specs=P("row", "col"),
        check_vma=False,
    )
```
